32 devices in a mesh: dp: 1, mp: 32 (over z, y, x, core).
Axes of the slice: x: 2, y: 2, z: 4, core: 2. Of those that a mesh axis runs over, the one named last changes fastest.
Arguments:
- layer_input: bfloat16 [1, 32, 16, 128, 128], P('dp', 'mp'), may hold values from -6 to 6
- cotangent: bfloat16 [1, 32, 16, 128, 128], P('dp', 'mp'), may hold values from -6 to 6
- spec_weight: bfloat16 [16, 16, 16, 2, 1024], P(None, None, None, None, 'mp'), may hold values from -1 to 1
- point_weight: bfloat16 [16, 16], replicated, may hold values from -1.5 to 1.5
- bias_term: float32 [16], replicated, may hold values from -3 to 3
Outputs:
- input_grad: bfloat16 [1, 32, 16, 128, 128], P('dp', 'mp')
- spec_grad: float32 [16, 16, 16, 2, 1024], P(None, None, None, None, 'mp')
- point_grad: float32 [16, 16], replicated
- bias_grad: float32 [16], replicated
The draws below stay inside these ranges and needn't reach their ends.
All inputs are finite; a program needn't handle non-finite values.
Results may differ from the reference program's by a relative error of at most 0.017.
Values may be sent and summed in bfloat16 or wider, within the bound.
A program may use at most 64 MiB of HBM per device.

```python
import math
import jax
import jax.numpy as jnp
from jax import lax

C = 16
MODES = 16
NX = 128
NY = 128
NZ = 32
BATCH = 1
SPECTRA = 1024


def steps_of(own_key, extent, shards, low, top_value):
    factor_of = 1.0
    for dim, blocks in shards:
        draws = jax.random.uniform(jax.random.fold_in(jax.random.fold_in(own_key, 6), dim), (blocks,), jnp.float32, low / len(shards), top_value / len(shards))
        factor_of = factor_of * jnp.repeat(jnp.exp(draws), extent[dim] // blocks).reshape((-1,) + (1,) * (len(extent) - 1 - dim))
    return factor_of


def centred(stream_key, shape, deviation, most, pieces=(), kind=jnp.bfloat16):
    level = steps_of(stream_key, shape, pieces, -0.22, 0.18) if pieces else 1.0
    result = jax.random.normal(stream_key, shape, jnp.float32) * deviation * level
    return jnp.minimum(jnp.maximum(result, -most), most).astype(kind)


def setup_inputs(seed: int = 0) -> dict:
    seeds = jax.random.split(jax.random.key(seed), 6)
    return {
        "layer_input": centred(seeds[0], (BATCH, NZ, C, NX, NY), 1.0, 6.0, ((1, 32),)),
        "cotangent": centred(seeds[1], (BATCH, NZ, C, NX, NY), 1.0, 6.0, ((1, 32),)),
        "spec_weight": centred(seeds[2], (MODES, C, C, 2, SPECTRA), (2 * C) ** -0.5, 1.0, ((4, 32),)),
        "point_weight": centred(seeds[3], (C, C), C ** -0.5, 1.5),
        "bias_term": centred(seeds[4], (C,), 0.5, 3.0, (), jnp.float32),
    }


SQRT_TWO_PI = math.sqrt(2.0 / math.pi)

def product(formula, first_op, second_op):
    return jnp.einsum(formula, first_op.astype(jnp.float32), second_op.astype(jnp.float32), precision=lax.Precision.HIGHEST)

def dft_table(length, freq_count, signed):
    frequency = jnp.arange(freq_count, dtype=jnp.int32)
    if signed:
        frequency = jnp.where(frequency >= freq_count // 2, frequency - freq_count, frequency)
    places = jnp.arange(length, dtype=jnp.int32)
    phases = jnp.mod(places[:, None] * frequency[None, :], length).astype(jnp.float32) * (2.0 * math.pi / length)
    return jnp.concatenate([jnp.cos(phases), -jnp.sin(phases)], axis=1).astype(jnp.bfloat16)

def to_spectrum(values, table_x, table_y, table_z, factor):
    depth_z, channels = (values.shape[0], values.shape[1])
    half_x = table_x.shape[1] // 2
    half_y = table_y.shape[1] // 2
    half_z = table_z.shape[1] // 2
    along_y = product('zcxy,yk->zcxk', values, table_y).astype(jnp.bfloat16)
    partial_value = product('zcxk,xa->zcak', along_y, table_x)
    real_part = partial_value[:, :, :half_x, :half_y] - partial_value[:, :, half_x:, half_y:]
    imag_part = partial_value[:, :, :half_x, half_y:] + partial_value[:, :, half_x:, :half_y]
    planes = jnp.stack([real_part, imag_part], axis=2).reshape(depth_z, channels, 2, half_x * half_y).astype(jnp.bfloat16)
    along_z = product('zcrp,zk->kcrp', planes, table_z)
    real_z = along_z[:half_z, :, 0] - along_z[half_z:, :, 1]
    imag_z = along_z[:half_z, :, 1] + along_z[half_z:, :, 0]
    return (factor * jnp.stack([real_z, imag_z], axis=2)).astype(jnp.bfloat16)

def to_field(spectrum, table_x, table_y, table_z, factor):
    depth_z = table_z.shape[0]
    half_z = table_z.shape[1] // 2
    cells_x = table_x.shape[0]
    half_x = table_x.shape[1] // 2
    half_y = table_y.shape[1] // 2
    waves_z = table_z.reshape(depth_z, 2, half_z)
    along_z = product('kcrp,zqk->zqcrp', spectrum, waves_z)
    real_z = along_z[:, 0, :, 0] + along_z[:, 1, :, 1]
    imag_z = along_z[:, 0, :, 1] - along_z[:, 1, :, 0]
    pencil_data = jnp.stack([real_z, imag_z], axis=2).astype(jnp.bfloat16)
    channels = pencil_data.shape[1]
    mode_grid = pencil_data.reshape(depth_z, channels, 2, half_x, half_y)
    along_x = product('zcrab,xqa->zcxqrb', mode_grid, table_x.reshape(cells_x, 2, half_x))
    real_x = along_x[:, :, :, 0, 0] + along_x[:, :, :, 1, 1]
    imag_x = along_x[:, :, :, 0, 1] - along_x[:, :, :, 1, 0]
    half_spec = jnp.concatenate([real_x, imag_x], axis=-1).astype(jnp.bfloat16)
    return factor * product('zcxk,yk->zcxy', half_spec, table_y)

def mix_modes(spectrum, weight, mode_scale):
    formula = 'kip,kiop->kop'
    spec_re, spec_im = (spectrum[:, :, 0], spectrum[:, :, 1])
    weight_re, weight_im = (weight[:, :, :, 0], weight[:, :, :, 1])
    real_part = product(formula, spec_re, weight_re) - product(formula, spec_im, weight_im)
    imag_part = product(formula, spec_re, weight_im) + product(formula, spec_im, weight_re)
    return (mode_scale[:, None, None, None] * jnp.stack([real_part, imag_part], axis=2)).astype(jnp.bfloat16)

def back_modes(grads, weight, mode_scale):
    formula = 'kop,kiop->kip'
    grad_re, grad_im = (grads[:, :, 0], grads[:, :, 1])
    weight_re, weight_im = (weight[:, :, :, 0], weight[:, :, :, 1])
    real_part = product(formula, grad_re, weight_re) + product(formula, grad_im, weight_im)
    imag_part = product(formula, grad_im, weight_re) - product(formula, grad_re, weight_im)
    return (mode_scale[:, None, None, None] * jnp.stack([real_part, imag_part], axis=2)).astype(jnp.bfloat16)

def gelu_slope(pre_act):
    inner_arg = SQRT_TWO_PI * (pre_act + 0.044715 * pre_act * pre_act * pre_act)
    tanh_val = jnp.tanh(inner_arg)
    return 0.5 * (1.0 + tanh_val) + 0.5 * pre_act * (1.0 - tanh_val * tanh_val) * SQRT_TWO_PI * (1.0 + 0.134145 * pre_act * pre_act)

def reference(layer_input, cotangent, spec_weight, point_weight, bias_term):
    depth_z, cells_x, cells_y = (layer_input.shape[1], layer_input.shape[3], layer_input.shape[4])
    mode_count = spec_weight.shape[0]
    table_x = dft_table(cells_x, 2 * mode_count, True)
    table_y = dft_table(cells_y, 2 * mode_count, True)
    table_z = dft_table(depth_z, mode_count, False)
    factor = 1.0 / math.sqrt(cells_x * cells_y * depth_z)
    mode_scale = jnp.where(jnp.arange(mode_count) == 0, 1.0, 2.0).astype(jnp.float32)

    def one_sample(sample_pair):
        values, tangent = sample_pair
        spectrum = to_spectrum(values, table_x, table_y, table_z, factor)
        mixed_spec = mix_modes(spectrum, spec_weight, mode_scale)
        spectral = to_field(mixed_spec, table_x, table_y, table_z, factor)
        pre_act = spectral + product('zixy,io->zoxy', values, point_weight) + bias_term[None, :, None, None]
        grad_pre = (tangent.astype(jnp.float32) * gelu_slope(pre_act)).astype(jnp.bfloat16)
        grad_spectrum = to_spectrum(grad_pre, table_x, table_y, table_z, factor)
        back_spec = back_modes(grad_spectrum, spec_weight, mode_scale)
        grad_values = (to_field(back_spec, table_x, table_y, table_z, factor) + product('zoxy,io->zixy', grad_pre, point_weight)).astype(jnp.bfloat16)
        point_terms = factor * product('zixy,zoxy->io', values, grad_pre)
        bias_terms = factor * lax.optimization_barrier(jnp.sum(grad_pre.astype(jnp.float32), axis=(0, 2, 3)))
        return (grad_values, spectrum, grad_spectrum, point_terms, bias_terms)
    input_grad, spectra, grad_spectra, point_terms, bias_terms = lax.map(one_sample, (layer_input, cotangent))
    formula = 'nkip,nkop->kiop'
    spec_re, spec_im = (spectra[:, :, :, 0], spectra[:, :, :, 1])
    grad_re, grad_im = (grad_spectra[:, :, :, 0], grad_spectra[:, :, :, 1])
    real_part = product(formula, spec_re, grad_re) + product(formula, spec_im, grad_im)
    imag_part = product(formula, spec_re, grad_im) - product(formula, spec_im, grad_re)
    spec_grad = mode_scale[:, None, None, None, None] * jnp.stack([real_part, imag_part], axis=3)
    return (input_grad, spec_grad, lax.optimization_barrier(jnp.sum(point_terms, axis=0)), lax.optimization_barrier(jnp.sum(bias_terms, axis=0)))
```

```python
import math

import jax
import jax.numpy as jnp
from jax import lax
from jax.sharding import PartitionSpec as P

SQRT_TWO_PI = math.sqrt(2.0 / math.pi)


def mixed_dot(formula, first_op, second_op):
    return jnp.einsum(formula, first_op, second_op, preferred_element_type=jnp.float32)


def dft_table(length, freq_count, signed):
    frequency = jnp.arange(freq_count, dtype=jnp.int32)
    if signed:
        frequency = jnp.where(frequency >= freq_count // 2, frequency - freq_count, frequency)
    places = jnp.arange(length, dtype=jnp.int32)
    phases = jnp.mod(places[:, None] * frequency[None, :], length).astype(jnp.float32) * (
        2.0 * math.pi / length
    )
    return jnp.concatenate([jnp.cos(phases), -jnp.sin(phases)], axis=1).astype(jnp.bfloat16)


def split3(value):
    high = value.astype(jnp.bfloat16)
    rest = value - high.astype(jnp.float32)
    mid = rest.astype(jnp.bfloat16)
    low = (rest - mid.astype(jnp.float32)).astype(jnp.bfloat16)
    return jnp.stack([high, mid, low])


def to_spectrum(values, table_x, table_y, table_z, factor, extra=None):
    samples, local_z, channels = (values.shape[0], values.shape[1], values.shape[2])
    half_x = table_x.shape[1] // 2
    half_y = table_y.shape[1] // 2
    half_z = table_z.shape[1] // 2
    along_y = mixed_dot("nzcxy,yk->nzcxk", values, table_y).astype(jnp.bfloat16)
    partial_value = mixed_dot("nzcxk,xa->nzcak", along_y, table_x)
    real_part = partial_value[..., :half_x, :half_y] - partial_value[..., half_x:, half_y:]
    imag_part = partial_value[..., :half_x, half_y:] + partial_value[..., half_x:, :half_y]
    planes = (
        jnp.stack([real_part, imag_part], axis=3)
        .reshape(samples, local_z, channels, 2, half_x * half_y)
        .astype(jnp.bfloat16)
    )
    shards_mp = lax.axis_size("mp")
    width = half_x * half_y // shards_mp
    total = None
    if extra is not None:
        size = extra.size
        cells = samples * local_z * channels * 2
        more = -(-3 * size // cells)
        flat = jnp.pad(split3(extra).reshape(-1), (0, cells * more - 3 * size))
        flat = jnp.broadcast_to(
            flat.reshape(samples, local_z, channels, 2, 1, more),
            (samples, local_z, channels, 2, shards_mp, more),
        )
        planes = jnp.concatenate(
            [planes.reshape(samples, local_z, channels, 2, shards_mp, width), flat], axis=5
        ).reshape(samples, local_z, channels, 2, shards_mp * (width + more))
    planes = lax.all_to_all(planes, "mp", split_axis=4, concat_axis=1, tiled=True)
    if extra is not None:
        tail = planes[..., width:].astype(jnp.float32)
        tail = tail.reshape(samples, shards_mp, local_z, channels, 2, more)
        tail = jnp.transpose(tail, (1, 0, 2, 3, 4, 5)).reshape(shards_mp, -1)
        total = jnp.sum(jnp.sum(tail, axis=0)[: 3 * size].reshape(3, size), axis=0)
        planes = planes[..., :width]
    whole_z = mixed_dot("nzcrp,zk->nkcrp", planes, table_z)
    real_z = whole_z[:, :half_z, :, 0] - whole_z[:, half_z:, :, 1]
    imag_z = whole_z[:, :half_z, :, 1] + whole_z[:, half_z:, :, 0]
    result = (factor * jnp.stack([real_z, imag_z], axis=3)).astype(jnp.bfloat16)
    return result if extra is None else (result, total)


def to_field(spectrum, table_x, table_y, table_z, factor):
    depth_z = table_z.shape[0]
    half_z = table_z.shape[1] // 2
    cells_x = table_x.shape[0]
    half_x = table_x.shape[1] // 2
    half_y = table_y.shape[1] // 2
    waves_z = table_z.reshape(depth_z, 2, half_z)
    whole_z = mixed_dot("nkcrp,zqk->nzqcrp", spectrum, waves_z)
    real_z = whole_z[:, :, 0, :, 0] + whole_z[:, :, 1, :, 1]
    imag_z = whole_z[:, :, 0, :, 1] - whole_z[:, :, 1, :, 0]
    pencil_data = jnp.stack([real_z, imag_z], axis=3).astype(jnp.bfloat16)
    waves_x = table_x.reshape(cells_x, 2, half_x)
    pencil_rows = lax.all_to_all(pencil_data, "mp", split_axis=1, concat_axis=4, tiled=True)
    samples = pencil_rows.shape[0]
    local_z = pencil_rows.shape[1]
    channels = pencil_rows.shape[2]
    mode_grid = pencil_rows.reshape(samples, local_z, channels, 2, half_x, half_y)
    along_x = mixed_dot("nzcrab,xqa->nzcxqrb", mode_grid, waves_x)
    real_x = along_x[:, :, :, :, 0, 0] + along_x[:, :, :, :, 1, 1]
    imag_x = along_x[:, :, :, :, 0, 1] - along_x[:, :, :, :, 1, 0]
    half_spec = jnp.concatenate([real_x, imag_x], axis=-1).astype(jnp.bfloat16)
    return factor * mixed_dot("nzcxk,yk->nzcxy", half_spec, table_y)


def mix_modes(spectrum, weight, mode_scale):
    formula = "nkip,kiop->nkop"
    spec_re, spec_im = (spectrum[:, :, :, 0], spectrum[:, :, :, 1])
    weight_re, weight_im = (weight[:, :, :, 0], weight[:, :, :, 1])
    real_part = mixed_dot(formula, spec_re, weight_re) - mixed_dot(formula, spec_im, weight_im)
    imag_part = mixed_dot(formula, spec_re, weight_im) + mixed_dot(formula, spec_im, weight_re)
    return (
        mode_scale[None, :, None, None, None] * jnp.stack([real_part, imag_part], axis=3)
    ).astype(jnp.bfloat16)


def back_modes(grads, weight, mode_scale):
    formula = "nkop,kiop->nkip"
    grad_re, grad_im = (grads[:, :, :, 0], grads[:, :, :, 1])
    weight_re, weight_im = (weight[:, :, :, 0], weight[:, :, :, 1])
    real_part = mixed_dot(formula, grad_re, weight_re) + mixed_dot(formula, grad_im, weight_im)
    imag_part = mixed_dot(formula, grad_im, weight_re) - mixed_dot(formula, grad_re, weight_im)
    return (
        mode_scale[None, :, None, None, None] * jnp.stack([real_part, imag_part], axis=3)
    ).astype(jnp.bfloat16)


def weight_terms(spectra, grads, mode_scale):
    formula = "nkip,nkop->kiop"
    spec_re, spec_im = (spectra[:, :, :, 0], spectra[:, :, :, 1])
    grad_re, grad_im = (grads[:, :, :, 0], grads[:, :, :, 1])
    real_part = mixed_dot(formula, spec_re, grad_re) + mixed_dot(formula, spec_im, grad_im)
    imag_part = mixed_dot(formula, spec_re, grad_im) - mixed_dot(formula, spec_im, grad_re)
    return mode_scale[:, None, None, None, None] * jnp.stack([real_part, imag_part], axis=3)


def gelu_slope(pre_act):
    inner_arg = SQRT_TWO_PI * (pre_act + 0.044715 * pre_act * pre_act * pre_act)
    tanh_val = jnp.tanh(inner_arg)
    return 0.5 * (1.0 + tanh_val) + 0.5 * pre_act * (1.0 - tanh_val * tanh_val) * SQRT_TWO_PI * (
        1.0 + 0.134145 * pre_act * pre_act
    )


def shards(layer_input, cotangent, spec_weight, point_weight, bias_term):
    local_z, cells_x, cells_y = (layer_input.shape[1], layer_input.shape[3], layer_input.shape[4])
    depth_z = local_z * lax.axis_size("mp")
    mode_count = spec_weight.shape[0]
    table_x = dft_table(cells_x, 2 * mode_count, True)
    table_y = dft_table(cells_y, 2 * mode_count, True)
    table_z = dft_table(depth_z, mode_count, False)
    factor = 1.0 / math.sqrt(cells_x * cells_y * depth_z)
    mode_scale = jnp.where(jnp.arange(mode_count) == 0, 1.0, 2.0).astype(jnp.float32)
    spectrum = to_spectrum(layer_input, table_x, table_y, table_z, factor)
    mixed_spec = mix_modes(spectrum, spec_weight, mode_scale)
    spectral = to_field(mixed_spec, table_x, table_y, table_z, factor)
    pre_act = (
        spectral
        + mixed_dot("nzixy,io->nzoxy", layer_input, point_weight)
        + bias_term[None, None, :, None, None]
    )
    grad_pre = (cotangent.astype(jnp.float32) * gelu_slope(pre_act)).astype(jnp.bfloat16)
    point_terms = factor * mixed_dot("nzixy,nzoxy->io", layer_input, grad_pre)
    bias_terms = factor * jnp.sum(grad_pre, axis=(0, 1, 3, 4), dtype=jnp.float32)
    terms = jnp.concatenate([point_terms, bias_terms[None]], axis=0)
    grad_spectrum, terms_sum = to_spectrum(
        grad_pre, table_x, table_y, table_z, factor, terms.reshape(-1)
    )
    terms_sum = lax.psum(terms_sum.reshape(terms.shape), "dp")
    point_grad, bias_grad = terms_sum[:-1], terms_sum[-1]
    back_spec = back_modes(grad_spectrum, spec_weight, mode_scale)
    input_grad = (
        to_field(back_spec, table_x, table_y, table_z, factor)
        + mixed_dot("nzoxy,io->nzixy", grad_pre, point_weight)
    ).astype(jnp.bfloat16)
    spec_grad = lax.psum(
        weight_terms(spectrum, grad_spectrum, mode_scale).astype(jnp.bfloat16), "dp"
    ).astype(jnp.float32)
    return (input_grad, spec_grad, point_grad, bias_grad)


def solution(mesh):
    placed = (
        P("dp", "mp", None, None, None),
        P("dp", "mp", None, None, None),
        P(None, None, None, None, "mp"),
        P(),
        P(),
    )
    return jax.shard_map(
        shards,
        mesh=mesh,
        in_specs=placed,
        out_specs=(P("dp", "mp", None, None, None), P(None, None, None, None, "mp"), P(), P()),
        check_vma=False,
    )
```

```python
import functools
import math

import jax
import jax.numpy as jnp
import ml_dtypes
import numpy as np
from jax import lax
from jax.experimental import pallas as pl
from jax.experimental.pallas import tpu as pltpu
from jax.sharding import PartitionSpec as P

SQRT_TWO_PI = math.sqrt(2.0 / math.pi)


def mixed_dot(formula, first_op, second_op):
    return jnp.einsum(formula, first_op, second_op, preferred_element_type=jnp.float32)


def dft_table(length, freq_count, signed):
    frequency = jnp.arange(freq_count, dtype=jnp.int32)
    if signed:
        frequency = jnp.where(frequency >= freq_count // 2, frequency - freq_count, frequency)
    places = jnp.arange(length, dtype=jnp.int32)
    phases = jnp.mod(places[:, None] * frequency[None, :], length).astype(jnp.float32) * (
        2.0 * math.pi / length
    )
    return jnp.concatenate([jnp.cos(phases), -jnp.sin(phases)], axis=1).astype(jnp.bfloat16)


def split3(value):
    high = value.astype(jnp.bfloat16)
    rest = value - high.astype(jnp.float32)
    mid = rest.astype(jnp.bfloat16)
    low = (rest - mid.astype(jnp.float32)).astype(jnp.bfloat16)
    return jnp.stack([high, mid, low])


def to_spectrum(values, table_x, table_y, table_z, factor, extra=None):
    samples, local_z, channels = (values.shape[0], values.shape[1], values.shape[2])
    half_x = table_x.shape[1] // 2
    half_y = table_y.shape[1] // 2
    half_z = table_z.shape[1] // 2
    along_y = mixed_dot("nzcxy,yk->nzcxk", values, table_y).astype(jnp.bfloat16)
    partial_value = mixed_dot("nzcxk,xa->nzcak", along_y, table_x)
    real_part = partial_value[..., :half_x, :half_y] - partial_value[..., half_x:, half_y:]
    imag_part = partial_value[..., :half_x, half_y:] + partial_value[..., half_x:, :half_y]
    planes = (
        jnp.stack([real_part, imag_part], axis=3)
        .reshape(samples, local_z, channels, 2, half_x * half_y)
        .astype(jnp.bfloat16)
    )
    shards_mp = lax.axis_size("mp")
    width = half_x * half_y // shards_mp
    total = None
    if extra is not None:
        size = extra.size
        cells = samples * local_z * channels * 2
        more = -(-3 * size // cells)
        flat = jnp.pad(split3(extra).reshape(-1), (0, cells * more - 3 * size))
        flat = jnp.broadcast_to(
            flat.reshape(samples, local_z, channels, 2, 1, more),
            (samples, local_z, channels, 2, shards_mp, more),
        )
        planes = jnp.concatenate(
            [planes.reshape(samples, local_z, channels, 2, shards_mp, width), flat], axis=5
        ).reshape(samples, local_z, channels, 2, shards_mp * (width + more))
    planes = lax.all_to_all(planes, "mp", split_axis=4, concat_axis=1, tiled=True)
    if extra is not None:
        tail = planes[..., width:].astype(jnp.float32)
        tail = tail.reshape(samples, shards_mp, local_z, channels, 2, more)
        tail = jnp.transpose(tail, (1, 0, 2, 3, 4, 5)).reshape(shards_mp, -1)
        total = jnp.sum(jnp.sum(tail, axis=0)[: 3 * size].reshape(3, size), axis=0)
        planes = planes[..., :width]
    whole_z = mixed_dot("nzcrp,zk->nkcrp", planes, table_z)
    real_z = whole_z[:, :half_z, :, 0] - whole_z[:, half_z:, :, 1]
    imag_z = whole_z[:, :half_z, :, 1] + whole_z[:, half_z:, :, 0]
    result = (factor * jnp.stack([real_z, imag_z], axis=3)).astype(jnp.bfloat16)
    return result if extra is None else (result, total)


def to_field(spectrum, table_x, table_y, table_z, factor):
    depth_z = table_z.shape[0]
    half_z = table_z.shape[1] // 2
    cells_x = table_x.shape[0]
    half_x = table_x.shape[1] // 2
    half_y = table_y.shape[1] // 2
    waves_z = table_z.reshape(depth_z, 2, half_z)
    whole_z = mixed_dot("nkcrp,zqk->nzqcrp", spectrum, waves_z)
    real_z = whole_z[:, :, 0, :, 0] + whole_z[:, :, 1, :, 1]
    imag_z = whole_z[:, :, 0, :, 1] - whole_z[:, :, 1, :, 0]
    pencil_data = jnp.stack([real_z, imag_z], axis=3).astype(jnp.bfloat16)
    waves_x = table_x.reshape(cells_x, 2, half_x)
    pencil_rows = lax.all_to_all(pencil_data, "mp", split_axis=1, concat_axis=4, tiled=True)
    samples = pencil_rows.shape[0]
    local_z = pencil_rows.shape[1]
    channels = pencil_rows.shape[2]
    mode_grid = pencil_rows.reshape(samples, local_z, channels, 2, half_x, half_y)
    along_x = mixed_dot("nzcrab,xqa->nzcxqrb", mode_grid, waves_x)
    real_x = along_x[:, :, :, :, 0, 0] + along_x[:, :, :, :, 1, 1]
    imag_x = along_x[:, :, :, :, 0, 1] - along_x[:, :, :, :, 1, 0]
    half_spec = jnp.concatenate([real_x, imag_x], axis=-1).astype(jnp.bfloat16)
    return factor * mixed_dot("nzcxk,yk->nzcxy", half_spec, table_y)


def mix_modes(spectrum, weight, mode_scale):
    formula = "nkip,kiop->nkop"
    spec_re, spec_im = (spectrum[:, :, :, 0], spectrum[:, :, :, 1])
    weight_re, weight_im = (weight[:, :, :, 0], weight[:, :, :, 1])
    real_part = mixed_dot(formula, spec_re, weight_re) - mixed_dot(formula, spec_im, weight_im)
    imag_part = mixed_dot(formula, spec_re, weight_im) + mixed_dot(formula, spec_im, weight_re)
    return (
        mode_scale[None, :, None, None, None] * jnp.stack([real_part, imag_part], axis=3)
    ).astype(jnp.bfloat16)


def back_modes(grads, weight, mode_scale):
    formula = "nkop,kiop->nkip"
    grad_re, grad_im = (grads[:, :, :, 0], grads[:, :, :, 1])
    weight_re, weight_im = (weight[:, :, :, 0], weight[:, :, :, 1])
    real_part = mixed_dot(formula, grad_re, weight_re) + mixed_dot(formula, grad_im, weight_im)
    imag_part = mixed_dot(formula, grad_im, weight_re) - mixed_dot(formula, grad_re, weight_im)
    return (
        mode_scale[None, :, None, None, None] * jnp.stack([real_part, imag_part], axis=3)
    ).astype(jnp.bfloat16)


def weight_terms(spectra, grads, mode_scale):
    formula = "nkip,nkop->kiop"
    spec_re, spec_im = (spectra[:, :, :, 0], spectra[:, :, :, 1])
    grad_re, grad_im = (grads[:, :, :, 0], grads[:, :, :, 1])
    real_part = mixed_dot(formula, spec_re, grad_re) + mixed_dot(formula, spec_im, grad_im)
    imag_part = mixed_dot(formula, spec_re, grad_im) - mixed_dot(formula, spec_im, grad_re)
    return mode_scale[:, None, None, None, None] * jnp.stack([real_part, imag_part], axis=3)


def gelu_slope(pre_act):
    inner_arg = SQRT_TWO_PI * (pre_act + 0.044715 * pre_act * pre_act * pre_act)
    tanh_val = jnp.tanh(inner_arg)
    return 0.5 * (1.0 + tanh_val) + 0.5 * pre_act * (1.0 - tanh_val * tanh_val) * SQRT_TWO_PI * (
        1.0 + 0.134145 * pre_act * pre_act
    )


def np_table(length, freq_count, signed):
    frequency = np.arange(freq_count)
    if signed:
        frequency = np.where(frequency >= freq_count // 2, frequency - freq_count, frequency)
    phases = np.mod(np.arange(length)[:, None] * frequency[None, :], length) * (
        2.0 * math.pi / length
    )
    return np.cos(phases), -np.sin(phases)


def lane_map(half, picks):
    out = np.zeros((4 * half, 4 * half))
    for group, (source, sign) in enumerate(picks):
        for lane in range(half):
            out[source * half + lane, group * half + lane] = sign
    return out


def fused_kernel(
    planes, chans, cx, cy, modes, factor,
    x_ref, cot_ref, w_ref, pw_ref, bias_ref,
    ty1, ty2, tyi, txf, txi, kf, ki, perm, mask_ref,
    dx_ref, sg_ref, term_ref,
    send, recv, fbuf, jbuf, spec, gspec, wraw, wa, mix, pwise, gp, bsum,
    send_sem, recv_sem,
):
    f32, bf16 = jnp.float32, jnp.bfloat16
    me = lax.axis_index("mp")
    n = planes
    half = 2 * modes
    kc = modes * chans
    blk = 16

    def dot(a, b):
        return jnp.dot(a, b, preferred_element_type=f32)

    barrier = pltpu.get_barrier_semaphore()

    def greet(j, carry):
        other = lax.rem(me + j, n)
        pl.semaphore_signal(
            barrier, inc=1, device_id={"mp": other}, device_id_type=pl.DeviceIdType.MESH
        )
        return carry

    lax.fori_loop(1, n, greet, 0)

    def ship(s):
        def go(j, carry):
            other = lax.rem(me + j, n)
            pltpu.make_async_remote_copy(
                src_ref=send.at[s, other],
                dst_ref=recv.at[s, me],
                send_sem=send_sem.at[s],
                recv_sem=recv_sem.at[s],
                device_id={"mp": other},
                device_id_type=pl.DeviceIdType.MESH,
            ).start()
            return carry

        lax.fori_loop(1, n, go, 0)
        recv[s, me] = send[s, me]

    def arrive(s):
        part = recv.at[s, pl.ds(0, n - 1)]
        pltpu.make_async_copy(part, part, recv_sem.at[s]).wait()

    def left(s):
        part = send.at[s, pl.ds(0, n - 1)]
        pltpu.make_async_copy(part, part, send_sem.at[s]).wait()

    def forward(src_ref, c):
        plane = src_ref[c]
        stacked = jnp.concatenate(
            [dot(plane, ty1[...]).astype(bf16), dot(plane, ty2[...]).astype(bf16)], axis=0
        )
        fbuf[:, c, :] = dot(txf[...], stacked)

    for c in range(chans):
        forward(x_ref, c)
    send[0] = fbuf[...].astype(bf16)
    pl.semaphore_wait(barrier, n - 1)
    ship(0)

    def spread(k, carry):
        rows = chans * chans
        start = k * (2 * rows)
        wraw[...] = w_ref[pl.ds(pl.multiple_of(start, 2 * rows), 2 * rows), :].astype(f32)
        real = wraw[pl.ds(0, rows, stride=2), :].astype(bf16)
        imag = wraw[pl.ds(1, rows, stride=2), :].astype(bf16)
        wa[k] = (dot(real, perm[5][:half]) + dot(imag, perm[6][:half])).astype(bf16).reshape(
            chans, chans, 4 * half
        )
        return carry

    lax.fori_loop(0, modes, spread, 0)

    row = lax.broadcasted_iota(jnp.int32, (chans * blk, chans), 0)
    col = lax.broadcasted_iota(jnp.int32, (chans * blk, chans), 1)
    rep = jnp.where(row // blk == col, 1.0, 0.0).astype(bf16)
    mask = mask_ref[...]
    kron_dims = (((1,), (1,)), ((), ()))

    def kron(transposed):
        if transposed:
            tall = lax.dot_general(rep, pw_ref[...], kron_dims, preferred_element_type=f32)
        else:
            tall = dot(rep, pw_ref[...])
        wide = lax.dot_general(tall.astype(bf16), rep, kron_dims, preferred_element_type=f32)
        return (wide * mask).astype(bf16)

    def pointwise(src_ref, matrix):
        for b in range(cx // blk):
            rows = pl.ds(b * blk, blk)
            block = src_ref[:, rows, :].reshape(chans * blk, cy)
            pwise[:, rows, :] = dot(matrix, block).reshape(chans, blk, cy)

    pointwise(x_ref, kron(True))

    def z_forward(s):
        got = recv[s].reshape(n * chans, 4 * half)
        turned = dot(got, perm[0]).astype(bf16)
        return (factor * (dot(kf[0], got) + dot(kf[1], turned))).astype(bf16)

    def z_inverse(s):
        folded = mix[...] + pltpu.roll(mix[...], 2 * half, 1)
        scale = jnp.where(
            lax.broadcasted_iota(jnp.int32, (kc, 4 * half), 0) < chans, 1.0, 2.0
        )
        modes_in = (scale * folded).astype(bf16)
        turned = dot(modes_in, perm[0]).astype(bf16)
        out = dot(ki[0], modes_in) - dot(ki[1], turned)
        send[s] = out.astype(bf16).reshape(n, chans, 4 * half)

    def prepare_inverse(s):
        got = recv[s].reshape(n * chans, 4 * half)
        fbuf[...] = recv[s].astype(f32)
        jbuf[...] = dot(got, perm[0]).reshape(n, chans, 4 * half)

    def inverse(c):
        pair = jnp.concatenate([fbuf[:, c, :], jbuf[:, c, :]], axis=0).astype(bf16)
        lines = dot(txi[...], pair).astype(bf16)
        return factor * dot(lines, tyi[...])

    arrive(0)
    spectrum = z_forward(0)
    spec[...] = dot(spectrum, perm[3])
    fold = dot(spectrum, perm[1])
    gspec[...] = fold

    def mixing(k, carry):
        rows = pl.ds(pl.multiple_of(k * chans, chans), chans)
        left_part = gspec[rows, :]
        mix[rows, :] = jnp.sum(left_part[:, None, :] * wa[k].astype(f32), axis=0)
        return carry

    lax.fori_loop(0, modes, mixing, 0)
    z_inverse(1)
    ship(1)
    arrive(1)
    prepare_inverse(1)
    for c in range(chans):
        pre = inverse(c) + pwise[c] + bias_ref[c]
        squared = pre * pre
        tanh_val = jnp.tanh(SQRT_TWO_PI * pre * (1.0 + 0.044715 * squared))
        slope = 0.5 * (1.0 + tanh_val) + (0.5 * SQRT_TWO_PI) * pre * (
            1.0 - tanh_val * tanh_val
        ) * (1.0 + 0.134145 * squared)
        grad = (cot_ref[c].astype(f32) * slope).astype(bf16)
        gp[c] = grad
        bsum[pl.ds(c, 1), :] = jnp.sum(grad.astype(f32), axis=0, keepdims=True)
    for c in range(chans):
        forward(gp, c)

    acc = jnp.zeros((chans * blk, chans * blk), f32)
    for b in range(cx // blk):
        rows = pl.ds(b * blk, blk)
        acc += lax.dot_general(
            x_ref[:, rows, :].reshape(chans * blk, cy),
            gp[:, rows, :].reshape(chans * blk, cy),
            kron_dims,
            preferred_element_type=f32,
        )
    short = jnp.sum((acc * mask).reshape(chans, blk, chans * blk), axis=1)
    lane_in = lax.broadcasted_iota(jnp.int32, (chans * blk, 4 * half), 0)
    lane_out = lax.broadcasted_iota(jnp.int32, (chans * blk, 4 * half), 1)
    gather = jnp.where(lane_in // blk == lane_out, 1.0, 0.0).astype(bf16)

    def split(value):
        high = value.astype(bf16)
        rest = value - high.astype(f32)
        mid = rest.astype(bf16)
        low = (rest - mid.astype(f32)).astype(bf16)
        return high, mid, low

    sums = sum(dot(piece, gather) for piece in split(short))
    bias_sum = jnp.sum(bsum[...], axis=1, keepdims=True)
    lanes = lax.broadcasted_iota(jnp.int32, (chans, 4 * half), 1)
    terms = factor * jnp.where(lanes == chans, bias_sum, sums)
    step = chans + 1
    block = jnp.zeros((chans, 4 * half), f32)
    for place, piece in enumerate(split(terms)):
        block += pltpu.roll(piece.astype(f32), 2 * half + place * step, 1)
    send[2] = (fbuf[...] + block[None]).astype(bf16)
    ship(2)
    pointwise(gp, kron(False))
    arrive(2)
    grad_spectrum = z_forward(2)
    gspec[...] = dot(grad_spectrum, perm[2])

    def back(k, carry):
        rows = pl.ds(pl.multiple_of(k * chans, chans), chans)
        mix[rows, :] = jnp.sum(gspec[rows, :][None] * wa[k].astype(f32), axis=1)
        return carry

    lax.fori_loop(0, modes, back, 0)
    z_inverse(3)
    ship(3)

    total = jnp.sum(recv[2].astype(f32), axis=0)
    joined = jnp.zeros_like(total)
    for place in range(3):
        joined += pltpu.roll(total, 2 * half - place * step, 1)
    term_ref[...] = joined
    gspec[...] = dot(grad_spectrum, perm[4])

    def outer(k, carry):
        rows = pl.ds(pl.multiple_of(k * chans, chans), chans)
        scale = jnp.where(k == 0, 1.0, 2.0)
        prod = (scale * spec[rows, :])[:, None, :] * gspec[rows, :][None]
        prod = prod.reshape(chans * chans, 4 * half)
        folded = prod + pltpu.roll(prod, 2 * half, 1)
        start = k * (2 * chans * chans)
        sg_ref[pl.ds(start, chans * chans, stride=2), :] = folded[:, :half]
        sg_ref[pl.ds(start + 1, chans * chans, stride=2), :] = folded[:, half : 2 * half]
        return carry

    lax.fori_loop(0, modes, outer, 0)
    arrive(3)
    prepare_inverse(3)
    for c in range(chans):
        dx_ref[c] = (inverse(c) + pwise[c]).astype(bf16)
    for s in range(4):
        left(s)


def fused(layer_input, cotangent, spec_weight, point_weight, bias_term):
    chans, cx, cy = layer_input.shape[2:]
    modes = spec_weight.shape[0]
    half = 2 * modes
    planes = lax.axis_size("mp")
    factor = 1.0 / math.sqrt(cx * cy * planes)
    kc = modes * chans
    rows = modes * chans * chans * 2

    def const(value):
        return jnp.asarray(np.asarray(value, np.float32).astype(ml_dtypes.bfloat16))

    cos_x, msin_x = np_table(cx, half, True)
    cos_y, msin_y = np_table(cy, half, True)
    cos_z, msin_z = np_table(planes, modes, False)
    zero_y = np.zeros_like(cos_y)
    eye = np.eye(chans)
    ty1 = np.concatenate([cos_y, msin_y, zero_y, zero_y], 1)
    ty2 = np.concatenate([-msin_y, cos_y, zero_y, zero_y], 1)
    tyi = ty1.T
    txf = np.concatenate([cos_x.T, msin_x.T], 1)
    txi = np.concatenate([cos_x, -msin_x], 1)
    kf = np.stack([np.kron(cos_z.T, eye), np.kron(msin_z.T, eye)])
    ki = np.stack([np.kron(cos_z, eye), np.kron(msin_z, eye)])
    perm = np.stack(
        [
            lane_map(half, [(1, -1), (0, 1), (0, 0), (0, 0)]),
            lane_map(half, [(0, 1), (1, 1), (1, 1), (0, 1)]),
            lane_map(half, [(0, 1), (1, 1), (1, -1), (0, -1)]),
            lane_map(half, [(0, 1), (0, 1), (1, 1), (1, 1)]),
            lane_map(half, [(0, 1), (1, 1), (1, 1), (0, -1)]),
            lane_map(half, [(0, 1), (0, 1), (0, 0), (0, 0)]),
            lane_map(half, [(0, 0), (0, 0), (0, -1), (0, 1)]),
        ]
    )
    mask = jnp.asarray(np.kron(np.ones((chans, chans)), np.eye(16)).astype(np.float32))
    vmem = pl.BlockSpec(memory_space=pltpu.VMEM)
    f32, bf16 = jnp.float32, jnp.bfloat16
    dx, sg, terms = pl.pallas_call(
        functools.partial(fused_kernel, planes, chans, cx, cy, modes, factor),
        out_shape=(
            jax.ShapeDtypeStruct((chans, cx, cy), bf16),
            jax.ShapeDtypeStruct((rows, half), f32),
            jax.ShapeDtypeStruct((chans, 4 * half), f32),
        ),
        in_specs=[vmem] * 4 + [pl.BlockSpec(memory_space=pltpu.SMEM)] + [vmem] * 9,
        out_specs=(vmem, vmem, vmem),
        scratch_shapes=[
            pltpu.VMEM((4, planes, chans, 4 * half), bf16),
            pltpu.VMEM((4, planes, chans, 4 * half), bf16),
            pltpu.VMEM((planes, chans, 4 * half), f32),
            pltpu.VMEM((planes, chans, 4 * half), f32),
            pltpu.VMEM((kc, 4 * half), f32),
            pltpu.VMEM((kc, 4 * half), f32),
            pltpu.VMEM((2 * chans * chans, half), f32),
            pltpu.VMEM((modes, chans, chans, 4 * half), bf16),
            pltpu.VMEM((kc, 4 * half), f32),
            pltpu.VMEM((chans, cx, cy), f32),
            pltpu.VMEM((chans, cx, cy), bf16),
            pltpu.VMEM((chans, cy), f32),
            pltpu.SemaphoreType.DMA((4,)),
            pltpu.SemaphoreType.DMA((4,)),
        ],
        compiler_params=pltpu.CompilerParams(
            collective_id=0, has_side_effects=True, vmem_limit_bytes=48 * 1024 * 1024
        ),
    )(
        layer_input.reshape(chans, cx, cy), cotangent.reshape(chans, cx, cy),
        spec_weight.reshape(rows, half), point_weight, bias_term,
        const(ty1), const(ty2), const(tyi), const(txf), const(txi), const(kf), const(ki),
        const(perm), mask,
    )
    return (
        dx.reshape(layer_input.shape),
        sg.reshape(spec_weight.shape),
        terms[:, :chans],
        terms[:, chans],
    )


def shards(layer_input, cotangent, spec_weight, point_weight, bias_term):
    local_z, cells_x, cells_y = (layer_input.shape[1], layer_input.shape[3], layer_input.shape[4])
    depth_z = local_z * lax.axis_size("mp")
    channels, half = (layer_input.shape[2], 2 * spec_weight.shape[0])
    one_row = spec_weight.shape[4] == half and lax.axis_size("mp") == half
    if (
        layer_input.shape[0] == 1 and local_z == 1 and lax.axis_size("dp") == 1
        and one_row and channels == 16 and half == 32 and cells_x == cells_y == 128
    ):
        return fused(layer_input, cotangent, spec_weight, point_weight, bias_term)
    mode_count = spec_weight.shape[0]
    table_x = dft_table(cells_x, 2 * mode_count, True)
    table_y = dft_table(cells_y, 2 * mode_count, True)
    table_z = dft_table(depth_z, mode_count, False)
    factor = 1.0 / math.sqrt(cells_x * cells_y * depth_z)
    mode_scale = jnp.where(jnp.arange(mode_count) == 0, 1.0, 2.0).astype(jnp.float32)
    spectrum = to_spectrum(layer_input, table_x, table_y, table_z, factor)
    mixed_spec = mix_modes(spectrum, spec_weight, mode_scale)
    spectral = to_field(mixed_spec, table_x, table_y, table_z, factor)
    pre_act = (
        spectral
        + mixed_dot("nzixy,io->nzoxy", layer_input, point_weight)
        + bias_term[None, None, :, None, None]
    )
    grad_pre = (cotangent.astype(jnp.float32) * gelu_slope(pre_act)).astype(jnp.bfloat16)
    point_terms = factor * mixed_dot("nzixy,nzoxy->io", layer_input, grad_pre)
    bias_terms = factor * jnp.sum(grad_pre, axis=(0, 1, 3, 4), dtype=jnp.float32)
    terms = jnp.concatenate([point_terms, bias_terms[None]], axis=0)
    grad_spectrum, terms_sum = to_spectrum(
        grad_pre, table_x, table_y, table_z, factor, terms.reshape(-1)
    )
    terms_sum = lax.psum(terms_sum.reshape(terms.shape), "dp")
    point_grad, bias_grad = terms_sum[:-1], terms_sum[-1]
    back_spec = back_modes(grad_spectrum, spec_weight, mode_scale)
    input_grad = (
        to_field(back_spec, table_x, table_y, table_z, factor)
        + mixed_dot("nzoxy,io->nzixy", grad_pre, point_weight)
    ).astype(jnp.bfloat16)
    spec_grad = lax.psum(
        weight_terms(spectrum, grad_spectrum, mode_scale).astype(jnp.bfloat16), "dp"
    ).astype(jnp.float32)
    return (input_grad, spec_grad, point_grad, bias_grad)


def solution(mesh):
    placed = (
        P("dp", "mp", None, None, None),
        P("dp", "mp", None, None, None),
        P(None, None, None, None, "mp"),
        P(),
        P(),
    )
    return jax.shard_map(
        shards,
        mesh=mesh,
        in_specs=placed,
        out_specs=(P("dp", "mp", None, None, None), P(None, None, None, None, "mp"), P(), P()),
        check_vma=False,
    )
```

```python
import functools
import math

import jax
import jax.numpy as jnp
import ml_dtypes
import numpy as np
from jax import lax
from jax.experimental import pallas as pl
from jax.experimental.pallas import tpu as pltpu
from jax.sharding import PartitionSpec as P

SQRT_TWO_PI = math.sqrt(2.0 / math.pi)


def mixed_dot(formula, first_op, second_op):
    return jnp.einsum(formula, first_op, second_op, preferred_element_type=jnp.float32)


def dft_table(length, freq_count, signed):
    frequency = jnp.arange(freq_count, dtype=jnp.int32)
    if signed:
        frequency = jnp.where(frequency >= freq_count // 2, frequency - freq_count, frequency)
    places = jnp.arange(length, dtype=jnp.int32)
    phases = jnp.mod(places[:, None] * frequency[None, :], length).astype(jnp.float32) * (
        2.0 * math.pi / length
    )
    return jnp.concatenate([jnp.cos(phases), -jnp.sin(phases)], axis=1).astype(jnp.bfloat16)


def split3(value):
    high = value.astype(jnp.bfloat16)
    rest = value - high.astype(jnp.float32)
    mid = rest.astype(jnp.bfloat16)
    low = (rest - mid.astype(jnp.float32)).astype(jnp.bfloat16)
    return jnp.stack([high, mid, low])


def to_spectrum(values, table_x, table_y, table_z, factor, extra=None):
    samples, local_z, channels = (values.shape[0], values.shape[1], values.shape[2])
    half_x = table_x.shape[1] // 2
    half_y = table_y.shape[1] // 2
    half_z = table_z.shape[1] // 2
    along_y = mixed_dot("nzcxy,yk->nzcxk", values, table_y).astype(jnp.bfloat16)
    partial_value = mixed_dot("nzcxk,xa->nzcak", along_y, table_x)
    real_part = partial_value[..., :half_x, :half_y] - partial_value[..., half_x:, half_y:]
    imag_part = partial_value[..., :half_x, half_y:] + partial_value[..., half_x:, :half_y]
    planes = (
        jnp.stack([real_part, imag_part], axis=3)
        .reshape(samples, local_z, channels, 2, half_x * half_y)
        .astype(jnp.bfloat16)
    )
    shards_mp = lax.axis_size("mp")
    width = half_x * half_y // shards_mp
    total = None
    if extra is not None:
        size = extra.size
        cells = samples * local_z * channels * 2
        more = -(-3 * size // cells)
        flat = jnp.pad(split3(extra).reshape(-1), (0, cells * more - 3 * size))
        flat = jnp.broadcast_to(
            flat.reshape(samples, local_z, channels, 2, 1, more),
            (samples, local_z, channels, 2, shards_mp, more),
        )
        planes = jnp.concatenate(
            [planes.reshape(samples, local_z, channels, 2, shards_mp, width), flat], axis=5
        ).reshape(samples, local_z, channels, 2, shards_mp * (width + more))
    planes = lax.all_to_all(planes, "mp", split_axis=4, concat_axis=1, tiled=True)
    if extra is not None:
        tail = planes[..., width:].astype(jnp.float32)
        tail = tail.reshape(samples, shards_mp, local_z, channels, 2, more)
        tail = jnp.transpose(tail, (1, 0, 2, 3, 4, 5)).reshape(shards_mp, -1)
        total = jnp.sum(jnp.sum(tail, axis=0)[: 3 * size].reshape(3, size), axis=0)
        planes = planes[..., :width]
    whole_z = mixed_dot("nzcrp,zk->nkcrp", planes, table_z)
    real_z = whole_z[:, :half_z, :, 0] - whole_z[:, half_z:, :, 1]
    imag_z = whole_z[:, :half_z, :, 1] + whole_z[:, half_z:, :, 0]
    result = (factor * jnp.stack([real_z, imag_z], axis=3)).astype(jnp.bfloat16)
    return result if extra is None else (result, total)


def to_field(spectrum, table_x, table_y, table_z, factor):
    depth_z = table_z.shape[0]
    half_z = table_z.shape[1] // 2
    cells_x = table_x.shape[0]
    half_x = table_x.shape[1] // 2
    half_y = table_y.shape[1] // 2
    waves_z = table_z.reshape(depth_z, 2, half_z)
    whole_z = mixed_dot("nkcrp,zqk->nzqcrp", spectrum, waves_z)
    real_z = whole_z[:, :, 0, :, 0] + whole_z[:, :, 1, :, 1]
    imag_z = whole_z[:, :, 0, :, 1] - whole_z[:, :, 1, :, 0]
    pencil_data = jnp.stack([real_z, imag_z], axis=3).astype(jnp.bfloat16)
    waves_x = table_x.reshape(cells_x, 2, half_x)
    pencil_rows = lax.all_to_all(pencil_data, "mp", split_axis=1, concat_axis=4, tiled=True)
    samples = pencil_rows.shape[0]
    local_z = pencil_rows.shape[1]
    channels = pencil_rows.shape[2]
    mode_grid = pencil_rows.reshape(samples, local_z, channels, 2, half_x, half_y)
    along_x = mixed_dot("nzcrab,xqa->nzcxqrb", mode_grid, waves_x)
    real_x = along_x[:, :, :, :, 0, 0] + along_x[:, :, :, :, 1, 1]
    imag_x = along_x[:, :, :, :, 0, 1] - along_x[:, :, :, :, 1, 0]
    half_spec = jnp.concatenate([real_x, imag_x], axis=-1).astype(jnp.bfloat16)
    return factor * mixed_dot("nzcxk,yk->nzcxy", half_spec, table_y)


def mix_modes(spectrum, weight, mode_scale):
    formula = "nkip,kiop->nkop"
    spec_re, spec_im = (spectrum[:, :, :, 0], spectrum[:, :, :, 1])
    weight_re, weight_im = (weight[:, :, :, 0], weight[:, :, :, 1])
    real_part = mixed_dot(formula, spec_re, weight_re) - mixed_dot(formula, spec_im, weight_im)
    imag_part = mixed_dot(formula, spec_re, weight_im) + mixed_dot(formula, spec_im, weight_re)
    return (
        mode_scale[None, :, None, None, None] * jnp.stack([real_part, imag_part], axis=3)
    ).astype(jnp.bfloat16)


def back_modes(grads, weight, mode_scale):
    formula = "nkop,kiop->nkip"
    grad_re, grad_im = (grads[:, :, :, 0], grads[:, :, :, 1])
    weight_re, weight_im = (weight[:, :, :, 0], weight[:, :, :, 1])
    real_part = mixed_dot(formula, grad_re, weight_re) + mixed_dot(formula, grad_im, weight_im)
    imag_part = mixed_dot(formula, grad_im, weight_re) - mixed_dot(formula, grad_re, weight_im)
    return (
        mode_scale[None, :, None, None, None] * jnp.stack([real_part, imag_part], axis=3)
    ).astype(jnp.bfloat16)


def weight_terms(spectra, grads, mode_scale):
    formula = "nkip,nkop->kiop"
    spec_re, spec_im = (spectra[:, :, :, 0], spectra[:, :, :, 1])
    grad_re, grad_im = (grads[:, :, :, 0], grads[:, :, :, 1])
    real_part = mixed_dot(formula, spec_re, grad_re) + mixed_dot(formula, spec_im, grad_im)
    imag_part = mixed_dot(formula, spec_re, grad_im) - mixed_dot(formula, spec_im, grad_re)
    return mode_scale[:, None, None, None, None] * jnp.stack([real_part, imag_part], axis=3)


def gelu_slope(pre_act):
    inner_arg = SQRT_TWO_PI * (pre_act + 0.044715 * pre_act * pre_act * pre_act)
    tanh_val = jnp.tanh(inner_arg)
    return 0.5 * (1.0 + tanh_val) + 0.5 * pre_act * (1.0 - tanh_val * tanh_val) * SQRT_TWO_PI * (
        1.0 + 0.134145 * pre_act * pre_act
    )


def np_table(length, freq_count, signed):
    frequency = np.arange(freq_count)
    if signed:
        frequency = np.where(frequency >= freq_count // 2, frequency - freq_count, frequency)
    phases = np.mod(np.arange(length)[:, None] * frequency[None, :], length) * (
        2.0 * math.pi / length
    )
    return np.cos(phases), -np.sin(phases)


def lane_map(half, picks):
    out = np.zeros((4 * half, 4 * half))
    for group, (source, sign) in enumerate(picks):
        for lane in range(half):
            out[source * half + lane, group * half + lane] = sign
    return out


def fused_kernel(
    planes, chans, cx, cy, modes, factor,
    x_hbm, cot_hbm, w_hbm, pw_hbm, bias_ref, *rest,
):
    tables_hbm, (dx_ref, spec, gout, term_ref), rest = rest[:9], rest[9:13], rest[13:]
    (send, recv, fbuf, jbuf, gspec, wraw, wa, mix, pwise, gp, bsum,
     send_sem, recv_sem, load_sem, x_ref, cot_ref, w_ref, pw_ref) = rest[:18]
    ty1, ty2, tyi, txf, txi, kf, ki, perm, mask_ref = rest[18:]
    loads = [
        pltpu.make_async_copy(source, target, load_sem.at[place])
        for place, (source, target) in enumerate(
            zip(
                (x_hbm, *(tables_hbm[t] for t in (0, 1, 3, 7, 8, 5)), w_hbm, pw_hbm,
                 cot_hbm, *(tables_hbm[t] for t in (2, 4, 6))),
                (x_ref, ty1, ty2, txf, perm, mask_ref, kf, w_ref, pw_ref,
                 cot_ref, tyi, txi, ki),
            )
        )
    ]
    for load in loads:
        load.start()
    f32, bf16 = jnp.float32, jnp.bfloat16
    me = lax.axis_index("mp")
    n = planes
    half = 2 * modes
    kc = modes * chans
    blk = 16

    def dot(a, b):
        return jnp.dot(a, b, preferred_element_type=f32)

    barrier = pltpu.get_barrier_semaphore()

    def greet(j, carry):
        other = lax.rem(me + j, n)
        pl.semaphore_signal(
            barrier, inc=1, device_id={"mp": other}, device_id_type=pl.DeviceIdType.MESH
        )
        return carry

    lax.fori_loop(1, n, greet, 0)

    def ship(s):
        def go(j, carry):
            other = lax.rem(me + j, n)
            pltpu.make_async_remote_copy(
                src_ref=send.at[s, other],
                dst_ref=recv.at[s, me],
                send_sem=send_sem.at[s],
                recv_sem=recv_sem.at[s],
                device_id={"mp": other},
                device_id_type=pl.DeviceIdType.MESH,
            ).start()
            return carry

        lax.fori_loop(1, n, go, 0)
        recv[s, me] = send[s, me]

    def arrive(s):
        part = recv.at[s, pl.ds(0, n - 1)]
        pltpu.make_async_copy(part, part, recv_sem.at[s]).wait()

    def left(s):
        part = send.at[s, pl.ds(0, n - 1)]
        pltpu.make_async_copy(part, part, send_sem.at[s]).wait()

    def forward(src_ref, c):
        plane = src_ref[c]
        stacked = jnp.concatenate(
            [dot(plane, ty1[...]).astype(bf16), dot(plane, ty2[...]).astype(bf16)], axis=0
        )
        fbuf[:, c, :] = dot(txf[...], stacked)

    for load in loads[:4]:
        load.wait()
    for c in range(chans):
        forward(x_ref, c)
    send[0] = fbuf[...].astype(bf16)
    pl.semaphore_wait(barrier, n - 1)
    ship(0)

    for load in loads[4:]:
        load.wait()

    def spread(k, carry):
        rows = chans * chans
        start = k * (2 * rows)
        wraw[...] = w_ref[pl.ds(pl.multiple_of(start, 2 * rows), 2 * rows), :].astype(f32)
        real = wraw[pl.ds(0, rows, stride=2), :].astype(bf16)
        imag = wraw[pl.ds(1, rows, stride=2), :].astype(bf16)
        wa[k] = (dot(real, perm[5][:half]) + dot(imag, perm[6][:half])).astype(bf16).reshape(
            chans, chans, 4 * half
        )
        return carry

    lax.fori_loop(0, modes, spread, 0)

    row = lax.broadcasted_iota(jnp.int32, (chans * blk, chans), 0)
    col = lax.broadcasted_iota(jnp.int32, (chans * blk, chans), 1)
    rep = jnp.where(row // blk == col, 1.0, 0.0).astype(bf16)
    mask = mask_ref[...]
    kron_dims = (((1,), (1,)), ((), ()))

    def kron(transposed):
        if transposed:
            tall = lax.dot_general(rep, pw_ref[...], kron_dims, preferred_element_type=f32)
        else:
            tall = dot(rep, pw_ref[...])
        wide = lax.dot_general(tall.astype(bf16), rep, kron_dims, preferred_element_type=f32)
        return (wide * mask).astype(bf16)

    def pointwise(src_ref, matrix):
        for b in range(cx // blk):
            rows = pl.ds(b * blk, blk)
            block = src_ref[:, rows, :].reshape(chans * blk, cy)
            pwise[:, rows, :] = dot(matrix, block).reshape(chans, blk, cy)

    pointwise(x_ref, kron(True))

    def z_forward(s):
        got = recv[s].reshape(n * chans, 4 * half)
        turned = dot(got, perm[0]).astype(bf16)
        return (factor * (dot(kf[0], got) + dot(kf[1], turned))).astype(bf16)

    def z_inverse(s):
        folded = mix[...] + pltpu.roll(mix[...], 2 * half, 1)
        scale = jnp.where(
            lax.broadcasted_iota(jnp.int32, (kc, 4 * half), 0) < chans, 1.0, 2.0
        )
        modes_in = (scale * folded).astype(bf16)
        turned = dot(modes_in, perm[0]).astype(bf16)
        out = dot(ki[0], modes_in) - dot(ki[1], turned)
        send[s] = out.astype(bf16).reshape(n, chans, 4 * half)

    def prepare_inverse(s):
        got = recv[s].reshape(n * chans, 4 * half)
        fbuf[...] = recv[s].astype(f32)
        jbuf[...] = dot(got, perm[0]).reshape(n, chans, 4 * half)

    def inverse(c):
        pair = jnp.concatenate([fbuf[:, c, :], jbuf[:, c, :]], axis=0).astype(bf16)
        lines = dot(txi[...], pair).astype(bf16)
        return factor * dot(lines, tyi[...])

    arrive(0)
    spectrum = z_forward(0)
    spec[...] = dot(spectrum, perm[3])
    fold = dot(spectrum, perm[1])
    gspec[...] = fold

    def mixing(k, carry):
        rows = pl.ds(pl.multiple_of(k * chans, chans), chans)
        left_part = gspec[rows, :]
        mix[rows, :] = jnp.sum(left_part[:, None, :] * wa[k].astype(f32), axis=0)
        return carry

    lax.fori_loop(0, modes, mixing, 0)
    z_inverse(1)
    ship(1)
    arrive(1)
    prepare_inverse(1)
    for c in range(chans):
        pre = inverse(c) + pwise[c] + bias_ref[c]
        squared = pre * pre
        tanh_val = jnp.tanh(SQRT_TWO_PI * pre * (1.0 + 0.044715 * squared))
        slope = 0.5 * (1.0 + tanh_val) + (0.5 * SQRT_TWO_PI) * pre * (
            1.0 - tanh_val * tanh_val
        ) * (1.0 + 0.134145 * squared)
        grad = (cot_ref[c].astype(f32) * slope).astype(bf16)
        gp[c] = grad
        bsum[pl.ds(c, 1), :] = jnp.sum(grad.astype(f32), axis=0, keepdims=True)
    for c in range(chans):
        forward(gp, c)

    acc = jnp.zeros((chans * blk, chans * blk), f32)
    for b in range(cx // blk):
        rows = pl.ds(b * blk, blk)
        acc += lax.dot_general(
            x_ref[:, rows, :].reshape(chans * blk, cy),
            gp[:, rows, :].reshape(chans * blk, cy),
            kron_dims,
            preferred_element_type=f32,
        )
    short = jnp.sum((acc * mask).reshape(chans, blk, chans * blk), axis=1)
    lane_in = lax.broadcasted_iota(jnp.int32, (chans * blk, 4 * half), 0)
    lane_out = lax.broadcasted_iota(jnp.int32, (chans * blk, 4 * half), 1)
    gather = jnp.where(lane_in // blk == lane_out, 1.0, 0.0).astype(bf16)

    def split(value):
        high = value.astype(bf16)
        rest = value - high.astype(f32)
        mid = rest.astype(bf16)
        low = (rest - mid.astype(f32)).astype(bf16)
        return high, mid, low

    sums = sum(dot(piece, gather) for piece in split(short))
    bias_sum = jnp.sum(bsum[...], axis=1, keepdims=True)
    lanes = lax.broadcasted_iota(jnp.int32, (chans, 4 * half), 1)
    terms = factor * jnp.where(lanes == chans, bias_sum, sums)
    step = chans + 1
    block = jnp.zeros((chans, 4 * half), f32)
    for place, piece in enumerate(split(terms)):
        block += pltpu.roll(piece.astype(f32), 2 * half + place * step, 1)
    send[2] = (fbuf[...] + block[None]).astype(bf16)
    ship(2)
    pointwise(gp, kron(False))
    arrive(2)
    grad_spectrum = z_forward(2)
    gspec[...] = dot(grad_spectrum, perm[2])

    def back(k, carry):
        rows = pl.ds(pl.multiple_of(k * chans, chans), chans)
        mix[rows, :] = jnp.sum(gspec[rows, :][None] * wa[k].astype(f32), axis=1)
        return carry

    lax.fori_loop(0, modes, back, 0)
    z_inverse(3)
    ship(3)

    term_ref[...] = jnp.sum(recv[2].astype(f32), axis=0)
    gout[...] = dot(grad_spectrum, perm[4])
    arrive(3)
    prepare_inverse(3)
    for c in range(chans):
        dx_ref[c] = (inverse(c) + pwise[c]).astype(bf16)
    for s in range(4):
        left(s)


def outer_kernel(modes, chans, spec, gspec, term_ref, sg_ref, point_ref, bias_ref):
    half = 2 * modes
    k = pl.program_id(0)

    @pl.when(k == 0)
    def _():
        total = term_ref[...]
        joined = jnp.zeros_like(total)
        for place in range(3):
            joined += pltpu.roll(total, 2 * half - place * (chans + 1), 1)
        point_ref[...] = joined[:, :chans]
        row = lax.broadcasted_iota(jnp.int32, (chans, chans), 0)
        col = lax.broadcasted_iota(jnp.int32, (chans, chans), 1)
        bias_ref[...] = jnp.sum(
            jnp.where(row == col, joined[:, chans : chans + 1], 0.0), axis=0, keepdims=True
        )

    scale = jnp.where(k == 0, 1.0, 2.0)
    prod = (scale * spec[...])[:, None, :] * gspec[...][None]
    prod = prod.reshape(chans * chans, 4 * half)
    folded = prod + pltpu.roll(prod, 2 * half, 1)
    sg_ref[pl.ds(0, chans * chans, stride=2), :] = folded[:, :half]
    sg_ref[pl.ds(1, chans * chans, stride=2), :] = folded[:, half : 2 * half]


def fused(layer_input, cotangent, spec_weight, point_weight, bias_term):
    chans, cx, cy = layer_input.shape[2:]
    modes = spec_weight.shape[0]
    half = 2 * modes
    planes = lax.axis_size("mp")
    factor = 1.0 / math.sqrt(cx * cy * planes)
    kc = modes * chans
    rows = modes * chans * chans * 2

    def const(value):
        return jnp.asarray(np.asarray(value, np.float32).astype(ml_dtypes.bfloat16))

    cos_x, msin_x = np_table(cx, half, True)
    cos_y, msin_y = np_table(cy, half, True)
    cos_z, msin_z = np_table(planes, modes, False)
    zero_y = np.zeros_like(cos_y)
    eye = np.eye(chans)
    ty1 = np.concatenate([cos_y, msin_y, zero_y, zero_y], 1)
    ty2 = np.concatenate([-msin_y, cos_y, zero_y, zero_y], 1)
    tyi = ty1.T
    txf = np.concatenate([cos_x.T, msin_x.T], 1)
    txi = np.concatenate([cos_x, -msin_x], 1)
    kf = np.stack([np.kron(cos_z.T, eye), np.kron(msin_z.T, eye)])
    ki = np.stack([np.kron(cos_z, eye), np.kron(msin_z, eye)])
    perm = np.stack(
        [
            lane_map(half, [(1, -1), (0, 1), (0, 0), (0, 0)]),
            lane_map(half, [(0, 1), (1, 1), (1, 1), (0, 1)]),
            lane_map(half, [(0, 1), (1, 1), (1, -1), (0, -1)]),
            lane_map(half, [(0, 1), (0, 1), (1, 1), (1, 1)]),
            lane_map(half, [(0, 1), (1, 1), (1, 1), (0, -1)]),
            lane_map(half, [(0, 1), (0, 1), (0, 0), (0, 0)]),
            lane_map(half, [(0, 0), (0, 0), (0, -1), (0, 1)]),
        ]
    )
    mask = jnp.asarray(np.kron(np.ones((chans, chans)), np.eye(16)).astype(np.float32))
    tables = [const(t) for t in (ty1, ty2, tyi, txf, txi, kf, ki, perm)] + [mask]
    vmem = pl.BlockSpec(memory_space=pltpu.VMEM)
    hbm = pl.BlockSpec(memory_space=pltpu.HBM)
    smem = pl.BlockSpec(memory_space=pltpu.SMEM)
    f32, bf16 = jnp.float32, jnp.bfloat16
    dx, spec, gspec, terms = pl.pallas_call(
        functools.partial(fused_kernel, planes, chans, cx, cy, modes, factor),
        out_shape=(
            jax.ShapeDtypeStruct((chans, cx, cy), bf16),
            jax.ShapeDtypeStruct((kc, 4 * half), f32),
            jax.ShapeDtypeStruct((kc, 4 * half), f32),
            jax.ShapeDtypeStruct((chans, 4 * half), f32),
        ),
        in_specs=[hbm] * 4 + [smem] + [hbm] * 9,
        out_specs=(vmem, vmem, vmem, vmem),
        scratch_shapes=[
            pltpu.VMEM((4, planes, chans, 4 * half), bf16),
            pltpu.VMEM((4, planes, chans, 4 * half), bf16),
            pltpu.VMEM((planes, chans, 4 * half), f32),
            pltpu.VMEM((planes, chans, 4 * half), f32),
            pltpu.VMEM((kc, 4 * half), f32),
            pltpu.VMEM((2 * chans * chans, half), f32),
            pltpu.VMEM((modes, chans, chans, 4 * half), bf16),
            pltpu.VMEM((kc, 4 * half), f32),
            pltpu.VMEM((chans, cx, cy), f32),
            pltpu.VMEM((chans, cx, cy), bf16),
            pltpu.VMEM((chans, cy), f32),
            pltpu.SemaphoreType.DMA((4,)),
            pltpu.SemaphoreType.DMA((4,)),
            pltpu.SemaphoreType.DMA((13,)),
            pltpu.VMEM((chans, cx, cy), bf16),
            pltpu.VMEM((chans, cx, cy), bf16),
            pltpu.VMEM((rows, half), bf16),
            pltpu.VMEM((chans, chans), bf16),
        ]
        + [pltpu.VMEM(t.shape, t.dtype) for t in tables],
        compiler_params=pltpu.CompilerParams(
            collective_id=0, has_side_effects=True, vmem_limit_bytes=60 * 1024 * 1024
        ),
    )(
        layer_input.reshape(chans, cx, cy), cotangent.reshape(chans, cx, cy),
        spec_weight.reshape(rows, half), point_weight, bias_term, *tables,
    )
    lines = pl.BlockSpec((chans, 4 * half), lambda k: (k, 0))
    sg, point, bias = pl.pallas_call(
        functools.partial(outer_kernel, modes, chans),
        grid=(modes,),
        out_shape=(
            jax.ShapeDtypeStruct((rows, half), f32),
            jax.ShapeDtypeStruct((chans, chans), f32),
            jax.ShapeDtypeStruct((1, chans), f32),
        ),
        in_specs=[lines, lines, pl.BlockSpec((chans, 4 * half), lambda k: (0, 0))],
        out_specs=(
            pl.BlockSpec((rows // modes, half), lambda k: (k, 0)),
            pl.BlockSpec((chans, chans), lambda k: (0, 0)),
            pl.BlockSpec((1, chans), lambda k: (0, 0)),
        ),
    )(spec, gspec, terms)
    return (
        dx.reshape(layer_input.shape),
        sg.reshape(spec_weight.shape),
        point,
        bias.reshape(chans),
    )


def shards(layer_input, cotangent, spec_weight, point_weight, bias_term):
    local_z, cells_x, cells_y = (layer_input.shape[1], layer_input.shape[3], layer_input.shape[4])
    depth_z = local_z * lax.axis_size("mp")
    channels, half = (layer_input.shape[2], 2 * spec_weight.shape[0])
    one_row = spec_weight.shape[4] == half and lax.axis_size("mp") == half
    if (
        layer_input.shape[0] == 1 and local_z == 1 and lax.axis_size("dp") == 1
        and one_row and channels == 16 and half == 32 and cells_x == cells_y == 128
    ):
        return fused(layer_input, cotangent, spec_weight, point_weight, bias_term)
    mode_count = spec_weight.shape[0]
    table_x = dft_table(cells_x, 2 * mode_count, True)
    table_y = dft_table(cells_y, 2 * mode_count, True)
    table_z = dft_table(depth_z, mode_count, False)
    factor = 1.0 / math.sqrt(cells_x * cells_y * depth_z)
    mode_scale = jnp.where(jnp.arange(mode_count) == 0, 1.0, 2.0).astype(jnp.float32)
    spectrum = to_spectrum(layer_input, table_x, table_y, table_z, factor)
    mixed_spec = mix_modes(spectrum, spec_weight, mode_scale)
    spectral = to_field(mixed_spec, table_x, table_y, table_z, factor)
    pre_act = (
        spectral
        + mixed_dot("nzixy,io->nzoxy", layer_input, point_weight)
        + bias_term[None, None, :, None, None]
    )
    grad_pre = (cotangent.astype(jnp.float32) * gelu_slope(pre_act)).astype(jnp.bfloat16)
    point_terms = factor * mixed_dot("nzixy,nzoxy->io", layer_input, grad_pre)
    bias_terms = factor * jnp.sum(grad_pre, axis=(0, 1, 3, 4), dtype=jnp.float32)
    terms = jnp.concatenate([point_terms, bias_terms[None]], axis=0)
    grad_spectrum, terms_sum = to_spectrum(
        grad_pre, table_x, table_y, table_z, factor, terms.reshape(-1)
    )
    terms_sum = lax.psum(terms_sum.reshape(terms.shape), "dp")
    point_grad, bias_grad = terms_sum[:-1], terms_sum[-1]
    back_spec = back_modes(grad_spectrum, spec_weight, mode_scale)
    input_grad = (
        to_field(back_spec, table_x, table_y, table_z, factor)
        + mixed_dot("nzoxy,io->nzixy", grad_pre, point_weight)
    ).astype(jnp.bfloat16)
    spec_grad = lax.psum(
        weight_terms(spectrum, grad_spectrum, mode_scale).astype(jnp.bfloat16), "dp"
    ).astype(jnp.float32)
    return (input_grad, spec_grad, point_grad, bias_grad)


def solution(mesh):
    placed = (
        P("dp", "mp", None, None, None),
        P("dp", "mp", None, None, None),
        P(None, None, None, None, "mp"),
        P(),
        P(),
    )
    return jax.shard_map(
        shards,
        mesh=mesh,
        in_specs=placed,
        out_specs=(P("dp", "mp", None, None, None), P(None, None, None, None, "mp"), P(), P()),
        check_vma=False,
    )
```

```python
import functools
import math

import jax
import jax.numpy as jnp
import ml_dtypes
import numpy as np
from jax import lax
from jax.experimental import pallas as pl
from jax.experimental.pallas import tpu as pltpu
from jax.sharding import PartitionSpec as P

SQRT_TWO_PI = math.sqrt(2.0 / math.pi)


def mixed_dot(formula, first_op, second_op):
    return jnp.einsum(formula, first_op, second_op, preferred_element_type=jnp.float32)


def dft_table(length, freq_count, signed):
    frequency = jnp.arange(freq_count, dtype=jnp.int32)
    if signed:
        frequency = jnp.where(frequency >= freq_count // 2, frequency - freq_count, frequency)
    places = jnp.arange(length, dtype=jnp.int32)
    phases = jnp.mod(places[:, None] * frequency[None, :], length).astype(jnp.float32) * (
        2.0 * math.pi / length
    )
    return jnp.concatenate([jnp.cos(phases), -jnp.sin(phases)], axis=1).astype(jnp.bfloat16)


def split3(value):
    high = value.astype(jnp.bfloat16)
    rest = value - high.astype(jnp.float32)
    mid = rest.astype(jnp.bfloat16)
    low = (rest - mid.astype(jnp.float32)).astype(jnp.bfloat16)
    return jnp.stack([high, mid, low])


def to_spectrum(values, table_x, table_y, table_z, factor, extra=None):
    samples, local_z, channels = (values.shape[0], values.shape[1], values.shape[2])
    half_x = table_x.shape[1] // 2
    half_y = table_y.shape[1] // 2
    half_z = table_z.shape[1] // 2
    along_y = mixed_dot("nzcxy,yk->nzcxk", values, table_y).astype(jnp.bfloat16)
    partial_value = mixed_dot("nzcxk,xa->nzcak", along_y, table_x)
    real_part = partial_value[..., :half_x, :half_y] - partial_value[..., half_x:, half_y:]
    imag_part = partial_value[..., :half_x, half_y:] + partial_value[..., half_x:, :half_y]
    planes = (
        jnp.stack([real_part, imag_part], axis=3)
        .reshape(samples, local_z, channels, 2, half_x * half_y)
        .astype(jnp.bfloat16)
    )
    shards_mp = lax.axis_size("mp")
    width = half_x * half_y // shards_mp
    total = None
    if extra is not None:
        size = extra.size
        cells = samples * local_z * channels * 2
        more = -(-3 * size // cells)
        flat = jnp.pad(split3(extra).reshape(-1), (0, cells * more - 3 * size))
        flat = jnp.broadcast_to(
            flat.reshape(samples, local_z, channels, 2, 1, more),
            (samples, local_z, channels, 2, shards_mp, more),
        )
        planes = jnp.concatenate(
            [planes.reshape(samples, local_z, channels, 2, shards_mp, width), flat], axis=5
        ).reshape(samples, local_z, channels, 2, shards_mp * (width + more))
    planes = lax.all_to_all(planes, "mp", split_axis=4, concat_axis=1, tiled=True)
    if extra is not None:
        tail = planes[..., width:].astype(jnp.float32)
        tail = tail.reshape(samples, shards_mp, local_z, channels, 2, more)
        tail = jnp.transpose(tail, (1, 0, 2, 3, 4, 5)).reshape(shards_mp, -1)
        total = jnp.sum(jnp.sum(tail, axis=0)[: 3 * size].reshape(3, size), axis=0)
        planes = planes[..., :width]
    whole_z = mixed_dot("nzcrp,zk->nkcrp", planes, table_z)
    real_z = whole_z[:, :half_z, :, 0] - whole_z[:, half_z:, :, 1]
    imag_z = whole_z[:, :half_z, :, 1] + whole_z[:, half_z:, :, 0]
    result = (factor * jnp.stack([real_z, imag_z], axis=3)).astype(jnp.bfloat16)
    return result if extra is None else (result, total)


def to_field(spectrum, table_x, table_y, table_z, factor):
    depth_z = table_z.shape[0]
    half_z = table_z.shape[1] // 2
    cells_x = table_x.shape[0]
    half_x = table_x.shape[1] // 2
    half_y = table_y.shape[1] // 2
    waves_z = table_z.reshape(depth_z, 2, half_z)
    whole_z = mixed_dot("nkcrp,zqk->nzqcrp", spectrum, waves_z)
    real_z = whole_z[:, :, 0, :, 0] + whole_z[:, :, 1, :, 1]
    imag_z = whole_z[:, :, 0, :, 1] - whole_z[:, :, 1, :, 0]
    pencil_data = jnp.stack([real_z, imag_z], axis=3).astype(jnp.bfloat16)
    waves_x = table_x.reshape(cells_x, 2, half_x)
    pencil_rows = lax.all_to_all(pencil_data, "mp", split_axis=1, concat_axis=4, tiled=True)
    samples = pencil_rows.shape[0]
    local_z = pencil_rows.shape[1]
    channels = pencil_rows.shape[2]
    mode_grid = pencil_rows.reshape(samples, local_z, channels, 2, half_x, half_y)
    along_x = mixed_dot("nzcrab,xqa->nzcxqrb", mode_grid, waves_x)
    real_x = along_x[:, :, :, :, 0, 0] + along_x[:, :, :, :, 1, 1]
    imag_x = along_x[:, :, :, :, 0, 1] - along_x[:, :, :, :, 1, 0]
    half_spec = jnp.concatenate([real_x, imag_x], axis=-1).astype(jnp.bfloat16)
    return factor * mixed_dot("nzcxk,yk->nzcxy", half_spec, table_y)


def mix_modes(spectrum, weight, mode_scale):
    formula = "nkip,kiop->nkop"
    spec_re, spec_im = (spectrum[:, :, :, 0], spectrum[:, :, :, 1])
    weight_re, weight_im = (weight[:, :, :, 0], weight[:, :, :, 1])
    real_part = mixed_dot(formula, spec_re, weight_re) - mixed_dot(formula, spec_im, weight_im)
    imag_part = mixed_dot(formula, spec_re, weight_im) + mixed_dot(formula, spec_im, weight_re)
    return (
        mode_scale[None, :, None, None, None] * jnp.stack([real_part, imag_part], axis=3)
    ).astype(jnp.bfloat16)


def back_modes(grads, weight, mode_scale):
    formula = "nkop,kiop->nkip"
    grad_re, grad_im = (grads[:, :, :, 0], grads[:, :, :, 1])
    weight_re, weight_im = (weight[:, :, :, 0], weight[:, :, :, 1])
    real_part = mixed_dot(formula, grad_re, weight_re) + mixed_dot(formula, grad_im, weight_im)
    imag_part = mixed_dot(formula, grad_im, weight_re) - mixed_dot(formula, grad_re, weight_im)
    return (
        mode_scale[None, :, None, None, None] * jnp.stack([real_part, imag_part], axis=3)
    ).astype(jnp.bfloat16)


def weight_terms(spectra, grads, mode_scale):
    formula = "nkip,nkop->kiop"
    spec_re, spec_im = (spectra[:, :, :, 0], spectra[:, :, :, 1])
    grad_re, grad_im = (grads[:, :, :, 0], grads[:, :, :, 1])
    real_part = mixed_dot(formula, spec_re, grad_re) + mixed_dot(formula, spec_im, grad_im)
    imag_part = mixed_dot(formula, spec_re, grad_im) - mixed_dot(formula, spec_im, grad_re)
    return mode_scale[:, None, None, None, None] * jnp.stack([real_part, imag_part], axis=3)


def gelu_slope(pre_act):
    inner_arg = SQRT_TWO_PI * (pre_act + 0.044715 * pre_act * pre_act * pre_act)
    tanh_val = jnp.tanh(inner_arg)
    return 0.5 * (1.0 + tanh_val) + 0.5 * pre_act * (1.0 - tanh_val * tanh_val) * SQRT_TWO_PI * (
        1.0 + 0.134145 * pre_act * pre_act
    )


def np_table(length, freq_count, signed):
    frequency = np.arange(freq_count)
    if signed:
        frequency = np.where(frequency >= freq_count // 2, frequency - freq_count, frequency)
    phases = np.mod(np.arange(length)[:, None] * frequency[None, :], length) * (
        2.0 * math.pi / length
    )
    return np.cos(phases), -np.sin(phases)


def lane_map(half, picks):
    out = np.zeros((4 * half, 4 * half))
    for group, (source, sign) in enumerate(picks):
        for lane in range(half):
            out[source * half + lane, group * half + lane] = sign
    return out


def fused_kernel(
    planes, chans, cx, cy, modes, factor,
    x_hbm, cot_hbm, w_hbm, pw_hbm, bias_ref, *rest,
):
    tables_hbm, (dx_ref, spec, gout, term_ref), rest = rest[:9], rest[9:13], rest[13:]
    (send, recv, fbuf, jbuf, gspec, wraw, wa, mix, pwise, gp, bsum,
     send_sem, recv_sem, load_sem, x_ref, cot_ref, w_ref, pw_ref,
     tsend, trecv) = rest[:20]
    ty1, ty2, tyi, txf, txi, kf, ki, perm, mask_ref = rest[20:]
    loads = [
        pltpu.make_async_copy(source, target, load_sem.at[place])
        for place, (source, target) in enumerate(
            zip(
                (x_hbm, *(tables_hbm[t] for t in (0, 1, 3, 7, 8, 5)), w_hbm, pw_hbm,
                 cot_hbm, *(tables_hbm[t] for t in (2, 4, 6))),
                (x_ref, ty1, ty2, txf, perm, mask_ref, kf, w_ref, pw_ref,
                 cot_ref, tyi, txi, ki),
            )
        )
    ]
    for load in loads:
        load.start()
    f32, bf16 = jnp.float32, jnp.bfloat16
    me = lax.axis_index("mp")
    n = planes
    half = 2 * modes
    kc = modes * chans
    blk = 16
    pair_rows = chans // 2

    def dot(a, b):
        return jnp.dot(a, b, preferred_element_type=f32)

    barrier = pltpu.get_barrier_semaphore()

    def greet(j, carry):
        other = lax.rem(me + j, n)
        pl.semaphore_signal(
            barrier, inc=1, device_id={"mp": other}, device_id_type=pl.DeviceIdType.MESH
        )
        return carry

    lax.fori_loop(1, n, greet, 0)

    def ship(s):
        def go(j, carry):
            other = lax.rem(me + j, n)
            pltpu.make_async_remote_copy(
                src_ref=send.at[s, other],
                dst_ref=recv.at[s, me],
                send_sem=send_sem.at[s],
                recv_sem=recv_sem.at[s],
                device_id={"mp": other},
                device_id_type=pl.DeviceIdType.MESH,
            ).start()
            return carry

        lax.fori_loop(1, n, go, 0)
        recv[s, me] = send[s, me]

    def spread_terms():
        def go(j, carry):
            other = lax.rem(me + j, n)
            pltpu.make_async_remote_copy(
                src_ref=tsend,
                dst_ref=trecv.at[me],
                send_sem=send_sem.at[4],
                recv_sem=recv_sem.at[4],
                device_id={"mp": other},
                device_id_type=pl.DeviceIdType.MESH,
            ).start()
            return carry

        lax.fori_loop(1, n, go, 0)
        trecv[me] = tsend[...]

    def arrive(s):
        part = recv.at[s, pl.ds(0, n - 1)]
        pltpu.make_async_copy(part, part, recv_sem.at[s]).wait()

    def left(s):
        part = send.at[s, pl.ds(0, n - 1)]
        pltpu.make_async_copy(part, part, send_sem.at[s]).wait()

    def forward(src_ref, c):
        plane = jnp.concatenate([src_ref[c], src_ref[c + pair_rows]], axis=1)
        stacked = jnp.concatenate(
            [dot(plane, ty1[...]).astype(bf16), dot(plane, ty2[...]).astype(bf16)], axis=0
        )
        fbuf[:, c, :] = dot(txf[...], stacked)

    for load in loads[:4]:
        load.wait()
    for c in range(pair_rows):
        forward(x_ref, c)
    send[0] = fbuf[...].astype(bf16)
    pl.semaphore_wait(barrier, n - 1)
    ship(0)

    for load in loads[4:]:
        load.wait()

    def spread(k, carry):
        rows = chans * chans
        start = k * (2 * rows)
        wraw[...] = w_ref[pl.ds(pl.multiple_of(start, 2 * rows), 2 * rows), :].astype(f32)
        real = wraw[pl.ds(0, rows, stride=2), :].astype(bf16)
        imag = wraw[pl.ds(1, rows, stride=2), :].astype(bf16)
        wa[k] = (dot(real, perm[5][:half]) + dot(imag, perm[6][:half])).astype(bf16).reshape(
            chans, chans, 4 * half
        )
        return carry

    lax.fori_loop(0, modes, spread, 0)

    row = lax.broadcasted_iota(jnp.int32, (chans * blk, chans), 0)
    col = lax.broadcasted_iota(jnp.int32, (chans * blk, chans), 1)
    rep = jnp.where(row // blk == col, 1.0, 0.0).astype(bf16)
    mask = mask_ref[...]
    kron_dims = (((1,), (1,)), ((), ()))

    def kron(transposed):
        if transposed:
            tall = lax.dot_general(rep, pw_ref[...], kron_dims, preferred_element_type=f32)
        else:
            tall = dot(rep, pw_ref[...])
        wide = lax.dot_general(tall.astype(bf16), rep, kron_dims, preferred_element_type=f32)
        return (wide * mask).astype(bf16)

    def pointwise(src_ref, matrix):
        for b in range(cx // blk):
            rows = pl.ds(b * blk, blk)
            block = src_ref[:, rows, :].reshape(chans * blk, cy)
            pwise[:, rows, :] = dot(matrix, block).reshape(chans, blk, cy)

    pointwise(x_ref, kron(True))

    def z_forward(s):
        got = recv[s].astype(f32).reshape(n * pair_rows, 4 * half).astype(bf16)
        turned = dot(got, perm[0]).astype(bf16)
        return (factor * (dot(kf[0], got) + dot(kf[1], turned))).astype(bf16)

    def z_inverse(s):
        folded = mix[...] + pltpu.roll(mix[...], 2 * half, 1)
        scale = jnp.where(
            lax.broadcasted_iota(jnp.int32, (kc, 4 * half), 0) < chans, 1.0, 2.0
        )
        folded = (scale * folded).reshape(modes, chans, 4 * half)
        lane = lax.broadcasted_iota(jnp.int32, (modes, pair_rows, 4 * half), 2)
        packed = jnp.where(lane < 2 * half, folded[:, :pair_rows], folded[:, pair_rows:])
        modes_in = packed.reshape(modes * pair_rows, 4 * half).astype(bf16)
        turned = dot(modes_in, perm[0]).astype(bf16)
        out = dot(ki[0], modes_in) - dot(ki[1], turned)
        send[s] = out.reshape(n, pair_rows, 4 * half).astype(bf16)

    def prepare_inverse(s):
        wide = recv[s].astype(f32)
        got = wide.reshape(n * pair_rows, 4 * half).astype(bf16)
        fbuf[...] = wide
        jbuf[...] = dot(got, perm[0]).reshape(n, pair_rows, 4 * half)

    def inverse(c):
        pair = jnp.concatenate([fbuf[:, c, :], jbuf[:, c, :]], axis=0).astype(bf16)
        lines = dot(txi[...], pair).astype(bf16)
        both = factor * dot(lines, tyi[...])
        return ((c, both[:, :cy]), (c + pair_rows, both[:, cy:]))

    def expand(values, which):
        parts = [
            dot(values, perm[which + 6 * h]).reshape(modes, pair_rows, 4 * half)
            for h in range(2)
        ]
        return jnp.concatenate(parts, axis=1).reshape(kc, 4 * half)

    arrive(0)
    spectrum = z_forward(0)
    spec[...] = expand(spectrum, 3)
    gspec[...] = expand(spectrum, 1)

    def mixing(k, carry):
        rows = pl.ds(pl.multiple_of(k * chans, chans), chans)
        left_part = gspec[rows, :]
        mix[rows, :] = jnp.sum(left_part[:, None, :] * wa[k].astype(f32), axis=0)
        return carry

    lax.fori_loop(0, modes, mixing, 0)
    z_inverse(1)
    ship(1)
    arrive(1)
    prepare_inverse(1)
    for c, spectral in (item for p in range(pair_rows) for item in inverse(p)):
        pre = spectral + pwise[c] + bias_ref[c]
        squared = pre * pre
        tanh_val = jnp.tanh(SQRT_TWO_PI * pre * (1.0 + 0.044715 * squared))
        slope = 0.5 * (1.0 + tanh_val) + (0.5 * SQRT_TWO_PI) * pre * (
            1.0 - tanh_val * tanh_val
        ) * (1.0 + 0.134145 * squared)
        grad = (cot_ref[c].astype(f32) * slope).astype(bf16)
        gp[c] = grad
        bsum[pl.ds(c, 1), :] = jnp.sum(grad.astype(f32), axis=0, keepdims=True)
    for c in range(pair_rows):
        forward(gp, c)
    send[2] = fbuf[...].astype(bf16)
    ship(2)
    pointwise(gp, kron(False))

    acc = jnp.zeros((chans * blk, chans * blk), f32)
    for b in range(cx // blk):
        rows = pl.ds(b * blk, blk)
        acc += lax.dot_general(
            x_ref[:, rows, :].reshape(chans * blk, cy),
            gp[:, rows, :].reshape(chans * blk, cy),
            kron_dims,
            preferred_element_type=f32,
        )
    short = jnp.sum((acc * mask).reshape(chans, blk, chans * blk), axis=1)
    lane_in = lax.broadcasted_iota(jnp.int32, (chans * blk, 4 * half), 0)
    lane_out = lax.broadcasted_iota(jnp.int32, (chans * blk, 4 * half), 1)
    gather = jnp.where(lane_in // blk == lane_out, 1.0, 0.0).astype(bf16)

    def split(value):
        high = value.astype(bf16)
        rest = value - high.astype(f32)
        mid = rest.astype(bf16)
        low = (rest - mid.astype(f32)).astype(bf16)
        return high, mid, low

    sums = sum(dot(piece, gather) for piece in split(short))
    bias_sum = jnp.sum(bsum[...], axis=1, keepdims=True)
    lanes = lax.broadcasted_iota(jnp.int32, (chans, 4 * half), 1)
    terms = factor * jnp.where(lanes == chans, bias_sum, sums)
    tsend[...] = terms[:pair_rows] + pltpu.roll(terms[pair_rows:], half, 1)
    spread_terms()
    arrive(2)
    grad_spectrum = z_forward(2)
    gspec[...] = expand(grad_spectrum, 2)

    def back(k, carry):
        rows = pl.ds(pl.multiple_of(k * chans, chans), chans)
        mix[rows, :] = jnp.sum(gspec[rows, :][None] * wa[k].astype(f32), axis=1)
        return carry

    lax.fori_loop(0, modes, back, 0)
    z_inverse(3)
    ship(3)

    gout[...] = expand(grad_spectrum, 4)
    every = trecv.at[pl.ds(0, n - 1)]
    pltpu.make_async_copy(every, every, recv_sem.at[4]).wait()
    term_ref[...] = jnp.sum(trecv[...], axis=0)
    arrive(3)
    prepare_inverse(3)
    for c, spectral in (item for p in range(pair_rows) for item in inverse(p)):
        dx_ref[c] = (spectral + pwise[c]).astype(bf16)
    for s in range(4):
        left(s)
    pltpu.make_async_copy(every, every, send_sem.at[4]).wait()


def outer_kernel(modes, chans, spec, gspec, term_ref, sg_hbm, point_ref, bias_ref, sg_ref, sems):
    half = 2 * modes
    area = 2 * chans * chans

    def put(k):
        rows = pl.ds(pl.multiple_of(k * area, area), area)
        return pltpu.make_async_copy(sg_ref.at[rows], sg_hbm.at[rows], sems.at[k])

    def outer(k, carry):
        rows = pl.ds(pl.multiple_of(k * chans, chans), chans)
        scale = jnp.where(k == 0, 1.0, 2.0)
        prod = (scale * spec[rows, :])[:, None, :] * gspec[rows, :][None]
        prod = prod.reshape(chans * chans, 4 * half)
        folded = prod + pltpu.roll(prod, 2 * half, 1)
        sg_ref[pl.ds(k * area, chans * chans, stride=2), :] = folded[:, :half]
        sg_ref[pl.ds(k * area + 1, chans * chans, stride=2), :] = folded[:, half : 2 * half]
        put(k).start()
        return carry

    lax.fori_loop(0, modes, outer, 0)
    total = term_ref[...]
    joined = jnp.concatenate([total, pltpu.roll(total, 3 * half, 1)], axis=0)
    point_ref[...] = joined[:, :chans]
    row = lax.broadcasted_iota(jnp.int32, (chans, chans), 0)
    col = lax.broadcasted_iota(jnp.int32, (chans, chans), 1)
    bias_ref[...] = jnp.sum(
        jnp.where(row == col, joined[:, chans : chans + 1], 0.0), axis=0, keepdims=True
    )

    def finish(k, carry):
        put(k).wait()
        return carry

    lax.fori_loop(0, modes, finish, 0)


def fused(layer_input, cotangent, spec_weight, point_weight, bias_term):
    chans, cx, cy = layer_input.shape[2:]
    modes = spec_weight.shape[0]
    half = 2 * modes
    planes = lax.axis_size("mp")
    factor = 1.0 / math.sqrt(cx * cy * planes)
    kc = modes * chans
    rows = modes * chans * chans * 2

    def const(value):
        return jnp.asarray(np.asarray(value, np.float32).astype(ml_dtypes.bfloat16))

    cos_x, msin_x = np_table(cx, half, True)
    cos_y, msin_y = np_table(cy, half, True)
    cos_z, msin_z = np_table(planes, modes, False)
    eye = np.eye(chans // 2)
    two = np.eye(2)
    ty1 = np.kron(two, np.concatenate([cos_y, msin_y], 1))
    ty2 = np.kron(two, np.concatenate([-msin_y, cos_y], 1))
    tyi = ty1.T
    txf = np.concatenate([cos_x.T, msin_x.T], 1)
    txi = np.concatenate([cos_x, -msin_x], 1)
    kf = np.stack([np.kron(cos_z.T, eye), np.kron(msin_z.T, eye)])
    ki = np.stack([np.kron(cos_z, eye), np.kron(msin_z, eye)])
    picks = (
        [(0, 1), (1, 1), (1, 1), (0, 1)],
        [(0, 1), (1, 1), (1, -1), (0, -1)],
        [(0, 1), (0, 1), (1, 1), (1, 1)],
        [(0, 1), (1, 1), (1, 1), (0, -1)],
    )
    perm = np.stack(
        [lane_map(half, [(1, -1), (0, 1), (3, -1), (2, 1)])]
        + [lane_map(half, pick) for pick in picks]
        + [
            lane_map(half, [(0, 1), (0, 1), (0, 0), (0, 0)]),
            lane_map(half, [(0, 0), (0, 0), (0, -1), (0, 1)]),
        ]
        + [lane_map(half, [(g + 2, sign) for g, sign in pick]) for pick in picks]
    )
    mask = jnp.asarray(np.kron(np.ones((chans, chans)), np.eye(16)).astype(np.float32))
    tables = [const(t) for t in (ty1, ty2, tyi, txf, txi, kf, ki, perm)] + [mask]
    vmem = pl.BlockSpec(memory_space=pltpu.VMEM)
    hbm = pl.BlockSpec(memory_space=pltpu.HBM)
    smem = pl.BlockSpec(memory_space=pltpu.SMEM)
    f32, bf16 = jnp.float32, jnp.bfloat16
    dx, spec, gspec, terms = pl.pallas_call(
        functools.partial(fused_kernel, planes, chans, cx, cy, modes, factor),
        out_shape=(
            jax.ShapeDtypeStruct((chans, cx, cy), bf16),
            jax.ShapeDtypeStruct((kc, 4 * half), f32),
            jax.ShapeDtypeStruct((kc, 4 * half), f32),
            jax.ShapeDtypeStruct((chans // 2, 4 * half), f32),
        ),
        in_specs=[hbm] * 4 + [smem] + [hbm] * 9,
        out_specs=(vmem, vmem, vmem, vmem),
        scratch_shapes=[
            pltpu.VMEM((4, planes, chans // 2, 4 * half), bf16),
            pltpu.VMEM((4, planes, chans // 2, 4 * half), bf16),
            pltpu.VMEM((planes, chans // 2, 4 * half), f32),
            pltpu.VMEM((planes, chans // 2, 4 * half), f32),
            pltpu.VMEM((kc, 4 * half), f32),
            pltpu.VMEM((2 * chans * chans, half), f32),
            pltpu.VMEM((modes, chans, chans, 4 * half), bf16),
            pltpu.VMEM((kc, 4 * half), f32),
            pltpu.VMEM((chans, cx, cy), f32),
            pltpu.VMEM((chans, cx, cy), bf16),
            pltpu.VMEM((chans, cy), f32),
            pltpu.SemaphoreType.DMA((5,)),
            pltpu.SemaphoreType.DMA((5,)),
            pltpu.SemaphoreType.DMA((13,)),
            pltpu.VMEM((chans, cx, cy), bf16),
            pltpu.VMEM((chans, cx, cy), bf16),
            pltpu.VMEM((rows, half), bf16),
            pltpu.VMEM((chans, chans), bf16),
            pltpu.VMEM((chans // 2, 4 * half), f32),
            pltpu.VMEM((planes, chans // 2, 4 * half), f32),
        ]
        + [pltpu.VMEM(t.shape, t.dtype) for t in tables],
        compiler_params=pltpu.CompilerParams(
            collective_id=0, has_side_effects=True, vmem_limit_bytes=60 * 1024 * 1024
        ),
    )(
        layer_input.reshape(chans, cx, cy), cotangent.reshape(chans, cx, cy),
        spec_weight.reshape(rows, half), point_weight, bias_term, *tables,
    )
    sg, point, bias = pl.pallas_call(
        functools.partial(outer_kernel, modes, chans),
        out_shape=(
            jax.ShapeDtypeStruct((rows, half), f32),
            jax.ShapeDtypeStruct((chans, chans), f32),
            jax.ShapeDtypeStruct((1, chans), f32),
        ),
        in_specs=[vmem] * 3,
        out_specs=(hbm, vmem, vmem),
        scratch_shapes=[pltpu.VMEM((rows, half), f32), pltpu.SemaphoreType.DMA((modes,))],
        compiler_params=pltpu.CompilerParams(vmem_limit_bytes=60 * 1024 * 1024),
    )(spec, gspec, terms)
    return (
        dx.reshape(layer_input.shape),
        sg.reshape(spec_weight.shape),
        point,
        bias.reshape(chans),
    )


def shards(layer_input, cotangent, spec_weight, point_weight, bias_term):
    local_z, cells_x, cells_y = (layer_input.shape[1], layer_input.shape[3], layer_input.shape[4])
    depth_z = local_z * lax.axis_size("mp")
    channels, half = (layer_input.shape[2], 2 * spec_weight.shape[0])
    one_row = spec_weight.shape[4] == half and lax.axis_size("mp") == half
    if (
        layer_input.shape[0] == 1 and local_z == 1 and lax.axis_size("dp") == 1
        and one_row and channels == 16 and half == 32 and cells_x == cells_y == 128
    ):
        return fused(layer_input, cotangent, spec_weight, point_weight, bias_term)
    mode_count = spec_weight.shape[0]
    table_x = dft_table(cells_x, 2 * mode_count, True)
    table_y = dft_table(cells_y, 2 * mode_count, True)
    table_z = dft_table(depth_z, mode_count, False)
    factor = 1.0 / math.sqrt(cells_x * cells_y * depth_z)
    mode_scale = jnp.where(jnp.arange(mode_count) == 0, 1.0, 2.0).astype(jnp.float32)
    spectrum = to_spectrum(layer_input, table_x, table_y, table_z, factor)
    mixed_spec = mix_modes(spectrum, spec_weight, mode_scale)
    spectral = to_field(mixed_spec, table_x, table_y, table_z, factor)
    pre_act = (
        spectral
        + mixed_dot("nzixy,io->nzoxy", layer_input, point_weight)
        + bias_term[None, None, :, None, None]
    )
    grad_pre = (cotangent.astype(jnp.float32) * gelu_slope(pre_act)).astype(jnp.bfloat16)
    point_terms = factor * mixed_dot("nzixy,nzoxy->io", layer_input, grad_pre)
    bias_terms = factor * jnp.sum(grad_pre, axis=(0, 1, 3, 4), dtype=jnp.float32)
    terms = jnp.concatenate([point_terms, bias_terms[None]], axis=0)
    grad_spectrum, terms_sum = to_spectrum(
        grad_pre, table_x, table_y, table_z, factor, terms.reshape(-1)
    )
    terms_sum = lax.psum(terms_sum.reshape(terms.shape), "dp")
    point_grad, bias_grad = terms_sum[:-1], terms_sum[-1]
    back_spec = back_modes(grad_spectrum, spec_weight, mode_scale)
    input_grad = (
        to_field(back_spec, table_x, table_y, table_z, factor)
        + mixed_dot("nzoxy,io->nzixy", grad_pre, point_weight)
    ).astype(jnp.bfloat16)
    spec_grad = lax.psum(
        weight_terms(spectrum, grad_spectrum, mode_scale).astype(jnp.bfloat16), "dp"
    ).astype(jnp.float32)
    return (input_grad, spec_grad, point_grad, bias_grad)


def solution(mesh):
    placed = (
        P("dp", "mp", None, None, None),
        P("dp", "mp", None, None, None),
        P(None, None, None, None, "mp"),
        P(),
        P(),
    )
    return jax.shard_map(
        shards,
        mesh=mesh,
        in_specs=placed,
        out_specs=(P("dp", "mp", None, None, None), P(None, None, None, None, "mp"), P(), P()),
        check_vma=False,
    )
```

```python
import functools
import math

import jax
import jax.numpy as jnp
import ml_dtypes
import numpy as np
from jax import lax
from jax.experimental import pallas as pl
from jax.experimental.pallas import tpu as pltpu
from jax.sharding import PartitionSpec as P

SQRT_TWO_PI = math.sqrt(2.0 / math.pi)


def mixed_dot(formula, first_op, second_op):
    return jnp.einsum(formula, first_op, second_op, preferred_element_type=jnp.float32)


def dft_table(length, freq_count, signed):
    frequency = jnp.arange(freq_count, dtype=jnp.int32)
    if signed:
        frequency = jnp.where(frequency >= freq_count // 2, frequency - freq_count, frequency)
    places = jnp.arange(length, dtype=jnp.int32)
    phases = jnp.mod(places[:, None] * frequency[None, :], length).astype(jnp.float32) * (
        2.0 * math.pi / length
    )
    return jnp.concatenate([jnp.cos(phases), -jnp.sin(phases)], axis=1).astype(jnp.bfloat16)


def split3(value):
    high = value.astype(jnp.bfloat16)
    rest = value - high.astype(jnp.float32)
    mid = rest.astype(jnp.bfloat16)
    low = (rest - mid.astype(jnp.float32)).astype(jnp.bfloat16)
    return jnp.stack([high, mid, low])


def to_spectrum(values, table_x, table_y, table_z, factor, extra=None):
    samples, local_z, channels = (values.shape[0], values.shape[1], values.shape[2])
    half_x = table_x.shape[1] // 2
    half_y = table_y.shape[1] // 2
    half_z = table_z.shape[1] // 2
    along_y = mixed_dot("nzcxy,yk->nzcxk", values, table_y).astype(jnp.bfloat16)
    partial_value = mixed_dot("nzcxk,xa->nzcak", along_y, table_x)
    real_part = partial_value[..., :half_x, :half_y] - partial_value[..., half_x:, half_y:]
    imag_part = partial_value[..., :half_x, half_y:] + partial_value[..., half_x:, :half_y]
    planes = (
        jnp.stack([real_part, imag_part], axis=3)
        .reshape(samples, local_z, channels, 2, half_x * half_y)
        .astype(jnp.bfloat16)
    )
    shards_mp = lax.axis_size("mp")
    width = half_x * half_y // shards_mp
    total = None
    if extra is not None:
        size = extra.size
        cells = samples * local_z * channels * 2
        more = -(-3 * size // cells)
        flat = jnp.pad(split3(extra).reshape(-1), (0, cells * more - 3 * size))
        flat = jnp.broadcast_to(
            flat.reshape(samples, local_z, channels, 2, 1, more),
            (samples, local_z, channels, 2, shards_mp, more),
        )
        planes = jnp.concatenate(
            [planes.reshape(samples, local_z, channels, 2, shards_mp, width), flat], axis=5
        ).reshape(samples, local_z, channels, 2, shards_mp * (width + more))
    planes = lax.all_to_all(planes, "mp", split_axis=4, concat_axis=1, tiled=True)
    if extra is not None:
        tail = planes[..., width:].astype(jnp.float32)
        tail = tail.reshape(samples, shards_mp, local_z, channels, 2, more)
        tail = jnp.transpose(tail, (1, 0, 2, 3, 4, 5)).reshape(shards_mp, -1)
        total = jnp.sum(jnp.sum(tail, axis=0)[: 3 * size].reshape(3, size), axis=0)
        planes = planes[..., :width]
    whole_z = mixed_dot("nzcrp,zk->nkcrp", planes, table_z)
    real_z = whole_z[:, :half_z, :, 0] - whole_z[:, half_z:, :, 1]
    imag_z = whole_z[:, :half_z, :, 1] + whole_z[:, half_z:, :, 0]
    result = (factor * jnp.stack([real_z, imag_z], axis=3)).astype(jnp.bfloat16)
    return result if extra is None else (result, total)


def to_field(spectrum, table_x, table_y, table_z, factor):
    depth_z = table_z.shape[0]
    half_z = table_z.shape[1] // 2
    cells_x = table_x.shape[0]
    half_x = table_x.shape[1] // 2
    half_y = table_y.shape[1] // 2
    waves_z = table_z.reshape(depth_z, 2, half_z)
    whole_z = mixed_dot("nkcrp,zqk->nzqcrp", spectrum, waves_z)
    real_z = whole_z[:, :, 0, :, 0] + whole_z[:, :, 1, :, 1]
    imag_z = whole_z[:, :, 0, :, 1] - whole_z[:, :, 1, :, 0]
    pencil_data = jnp.stack([real_z, imag_z], axis=3).astype(jnp.bfloat16)
    waves_x = table_x.reshape(cells_x, 2, half_x)
    pencil_rows = lax.all_to_all(pencil_data, "mp", split_axis=1, concat_axis=4, tiled=True)
    samples = pencil_rows.shape[0]
    local_z = pencil_rows.shape[1]
    channels = pencil_rows.shape[2]
    mode_grid = pencil_rows.reshape(samples, local_z, channels, 2, half_x, half_y)
    along_x = mixed_dot("nzcrab,xqa->nzcxqrb", mode_grid, waves_x)
    real_x = along_x[:, :, :, :, 0, 0] + along_x[:, :, :, :, 1, 1]
    imag_x = along_x[:, :, :, :, 0, 1] - along_x[:, :, :, :, 1, 0]
    half_spec = jnp.concatenate([real_x, imag_x], axis=-1).astype(jnp.bfloat16)
    return factor * mixed_dot("nzcxk,yk->nzcxy", half_spec, table_y)


def mix_modes(spectrum, weight, mode_scale):
    formula = "nkip,kiop->nkop"
    spec_re, spec_im = (spectrum[:, :, :, 0], spectrum[:, :, :, 1])
    weight_re, weight_im = (weight[:, :, :, 0], weight[:, :, :, 1])
    real_part = mixed_dot(formula, spec_re, weight_re) - mixed_dot(formula, spec_im, weight_im)
    imag_part = mixed_dot(formula, spec_re, weight_im) + mixed_dot(formula, spec_im, weight_re)
    return (
        mode_scale[None, :, None, None, None] * jnp.stack([real_part, imag_part], axis=3)
    ).astype(jnp.bfloat16)


def back_modes(grads, weight, mode_scale):
    formula = "nkop,kiop->nkip"
    grad_re, grad_im = (grads[:, :, :, 0], grads[:, :, :, 1])
    weight_re, weight_im = (weight[:, :, :, 0], weight[:, :, :, 1])
    real_part = mixed_dot(formula, grad_re, weight_re) + mixed_dot(formula, grad_im, weight_im)
    imag_part = mixed_dot(formula, grad_im, weight_re) - mixed_dot(formula, grad_re, weight_im)
    return (
        mode_scale[None, :, None, None, None] * jnp.stack([real_part, imag_part], axis=3)
    ).astype(jnp.bfloat16)


def weight_terms(spectra, grads, mode_scale):
    formula = "nkip,nkop->kiop"
    spec_re, spec_im = (spectra[:, :, :, 0], spectra[:, :, :, 1])
    grad_re, grad_im = (grads[:, :, :, 0], grads[:, :, :, 1])
    real_part = mixed_dot(formula, spec_re, grad_re) + mixed_dot(formula, spec_im, grad_im)
    imag_part = mixed_dot(formula, spec_re, grad_im) - mixed_dot(formula, spec_im, grad_re)
    return mode_scale[:, None, None, None, None] * jnp.stack([real_part, imag_part], axis=3)


def gelu_slope(pre_act):
    inner_arg = SQRT_TWO_PI * (pre_act + 0.044715 * pre_act * pre_act * pre_act)
    tanh_val = jnp.tanh(inner_arg)
    return 0.5 * (1.0 + tanh_val) + 0.5 * pre_act * (1.0 - tanh_val * tanh_val) * SQRT_TWO_PI * (
        1.0 + 0.134145 * pre_act * pre_act
    )


def np_table(length, freq_count, signed):
    frequency = np.arange(freq_count)
    if signed:
        frequency = np.where(frequency >= freq_count // 2, frequency - freq_count, frequency)
    phases = np.mod(np.arange(length)[:, None] * frequency[None, :], length) * (
        2.0 * math.pi / length
    )
    return np.cos(phases), -np.sin(phases)


def lane_map(half, picks):
    out = np.zeros((4 * half, 4 * half))
    for group, (source, sign) in enumerate(picks):
        for lane in range(half):
            out[source * half + lane, group * half + lane] = sign
    return out


def fused_kernel(
    planes, chans, cx, cy, modes, factor,
    x_hbm, cot_hbm, w_hbm, pw_hbm, bias_ref, *rest,
):
    tables_hbm, (got_ref, point_out, spec, gout, term_ref), rest = (
        rest[:9], rest[9:14], rest[14:]
    )
    (send, recv, fbuf, jbuf, gspec, wraw, wa, mix, pwise, gp, bsum,
     send_sem, recv_sem, load_sem, x_ref, cot_ref, w_ref, pw_ref,
     tsend, trecv) = rest[:20]
    ty1, ty2, tyi, txf, txi, kf, ki, perm, mask_ref = rest[20:]
    loads = [
        pltpu.make_async_copy(source, target, load_sem.at[place])
        for place, (source, target) in enumerate(
            zip(
                (x_hbm, *(tables_hbm[t] for t in (0, 1, 3, 7, 8, 5)), w_hbm, pw_hbm,
                 cot_hbm, *(tables_hbm[t] for t in (2, 4, 6))),
                (x_ref, ty1, ty2, txf, perm, mask_ref, kf, w_ref, pw_ref,
                 cot_ref, tyi, txi, ki),
            )
        )
    ]
    for load in loads:
        load.start()
    f32, bf16 = jnp.float32, jnp.bfloat16
    me = lax.axis_index("mp")
    n = planes
    half = 2 * modes
    kc = modes * chans
    blk = 16
    pair_rows = chans // 2

    def dot(a, b):
        return jnp.dot(a, b, preferred_element_type=f32)

    barrier = pltpu.get_barrier_semaphore()

    def greet(j, carry):
        other = lax.rem(me + j, n)
        pl.semaphore_signal(
            barrier, inc=1, device_id={"mp": other}, device_id_type=pl.DeviceIdType.MESH
        )
        return carry

    lax.fori_loop(1, n, greet, 0)

    def ship(s):
        def go(j, carry):
            other = lax.rem(me + j, n)
            pltpu.make_async_remote_copy(
                src_ref=send.at[s, other],
                dst_ref=recv.at[s, me],
                send_sem=send_sem.at[s],
                recv_sem=recv_sem.at[s],
                device_id={"mp": other},
                device_id_type=pl.DeviceIdType.MESH,
            ).start()
            return carry

        lax.fori_loop(1, n, go, 0)
        recv[s, me] = send[s, me]

    def spread_terms():
        def go(j, carry):
            other = lax.rem(me + j, n)
            pltpu.make_async_remote_copy(
                src_ref=tsend,
                dst_ref=trecv.at[me],
                send_sem=send_sem.at[4],
                recv_sem=recv_sem.at[4],
                device_id={"mp": other},
                device_id_type=pl.DeviceIdType.MESH,
            ).start()
            return carry

        lax.fori_loop(1, n, go, 0)
        trecv[me] = tsend[...]

    def arrive(s):
        part = recv.at[s, pl.ds(0, n - 1)]
        pltpu.make_async_copy(part, part, recv_sem.at[s]).wait()

    def left(s):
        part = send.at[s, pl.ds(0, n - 1)]
        pltpu.make_async_copy(part, part, send_sem.at[s]).wait()

    def forward(src_ref, c):
        plane = jnp.concatenate([src_ref[c], src_ref[c + pair_rows]], axis=1)
        stacked = jnp.concatenate(
            [dot(plane, ty1[...]).astype(bf16), dot(plane, ty2[...]).astype(bf16)], axis=0
        )
        fbuf[:, c, :] = dot(txf[...], stacked)

    for load in loads[:4]:
        load.wait()
    for c in range(pair_rows):
        forward(x_ref, c)
    send[0] = fbuf[...].astype(bf16)
    pl.semaphore_wait(barrier, n - 1)
    ship(0)

    for load in loads[4:]:
        load.wait()

    def spread(k, carry):
        rows = chans * chans
        start = k * (2 * rows)
        wraw[...] = w_ref[pl.ds(pl.multiple_of(start, 2 * rows), 2 * rows), :].astype(f32)
        real = wraw[pl.ds(0, rows, stride=2), :].astype(bf16)
        imag = wraw[pl.ds(1, rows, stride=2), :].astype(bf16)
        wa[k] = (dot(real, perm[5][:half]) + dot(imag, perm[6][:half])).astype(bf16).reshape(
            chans, chans, 4 * half
        )
        return carry

    lax.fori_loop(0, modes, spread, 0)

    row = lax.broadcasted_iota(jnp.int32, (chans * blk, chans), 0)
    col = lax.broadcasted_iota(jnp.int32, (chans * blk, chans), 1)
    rep = jnp.where(row // blk == col, 1.0, 0.0).astype(bf16)
    mask = mask_ref[...]
    kron_dims = (((1,), (1,)), ((), ()))

    def kron(transposed):
        if transposed:
            tall = lax.dot_general(rep, pw_ref[...], kron_dims, preferred_element_type=f32)
        else:
            tall = dot(rep, pw_ref[...])
        wide = lax.dot_general(tall.astype(bf16), rep, kron_dims, preferred_element_type=f32)
        return (wide * mask).astype(bf16)

    def pointwise(src_ref, matrix):
        for b in range(cx // blk):
            rows = pl.ds(b * blk, blk)
            block = src_ref[:, rows, :].reshape(chans * blk, cy)
            pwise[:, rows, :] = dot(matrix, block).reshape(chans, blk, cy)

    pointwise(x_ref, kron(True))

    def z_forward(s):
        got = recv[s].astype(f32).reshape(n * pair_rows, 4 * half).astype(bf16)
        turned = dot(got, perm[0]).astype(bf16)
        return (factor * (dot(kf[0], got) + dot(kf[1], turned))).astype(bf16)

    def z_inverse(s):
        folded = mix[...] + pltpu.roll(mix[...], 2 * half, 1)
        scale = jnp.where(
            lax.broadcasted_iota(jnp.int32, (kc, 4 * half), 0) < chans, 1.0, 2.0
        )
        folded = (scale * folded).reshape(modes, chans, 4 * half)
        lane = lax.broadcasted_iota(jnp.int32, (modes, pair_rows, 4 * half), 2)
        packed = jnp.where(lane < 2 * half, folded[:, :pair_rows], folded[:, pair_rows:])
        modes_in = packed.reshape(modes * pair_rows, 4 * half).astype(bf16)
        turned = dot(modes_in, perm[0]).astype(bf16)
        out = dot(ki[0], modes_in) - dot(ki[1], turned)
        send[s] = out.reshape(n, pair_rows, 4 * half).astype(bf16)

    def prepare_inverse(s):
        wide = recv[s].astype(f32)
        got = wide.reshape(n * pair_rows, 4 * half).astype(bf16)
        fbuf[...] = wide
        jbuf[...] = dot(got, perm[0]).reshape(n, pair_rows, 4 * half)

    def inverse(c):
        pair = jnp.concatenate([fbuf[:, c, :], jbuf[:, c, :]], axis=0).astype(bf16)
        lines = dot(txi[...], pair).astype(bf16)
        both = factor * dot(lines, tyi[...])
        return ((c, both[:, :cy]), (c + pair_rows, both[:, cy:]))

    def expand(values, which):
        parts = [
            dot(values, perm[which + 6 * h]).reshape(modes, pair_rows, 4 * half)
            for h in range(2)
        ]
        return jnp.concatenate(parts, axis=1).reshape(kc, 4 * half)

    arrive(0)
    spectrum = z_forward(0)
    spec[...] = expand(spectrum, 3)
    gspec[...] = expand(spectrum, 1)

    def mixing(k, carry):
        rows = pl.ds(pl.multiple_of(k * chans, chans), chans)
        left_part = gspec[rows, :]
        mix[rows, :] = jnp.sum(left_part[:, None, :] * wa[k].astype(f32), axis=0)
        return carry

    lax.fori_loop(0, modes, mixing, 0)
    z_inverse(1)
    ship(1)
    arrive(1)
    prepare_inverse(1)
    for c, spectral in (item for p in range(pair_rows) for item in inverse(p)):
        pre = spectral + pwise[c] + bias_ref[c]
        squared = pre * pre
        tanh_val = jnp.tanh(SQRT_TWO_PI * pre * (1.0 + 0.044715 * squared))
        slope = 0.5 * (1.0 + tanh_val) + (0.5 * SQRT_TWO_PI) * pre * (
            1.0 - tanh_val * tanh_val
        ) * (1.0 + 0.134145 * squared)
        grad = (cot_ref[c].astype(f32) * slope).astype(bf16)
        gp[c] = grad
        bsum[pl.ds(c, 1), :] = jnp.sum(grad.astype(f32), axis=0, keepdims=True)
    for c in range(pair_rows):
        forward(gp, c)
    send[2] = fbuf[...].astype(bf16)
    ship(2)
    pointwise(gp, kron(False))
    handed = pltpu.make_async_copy(pwise, point_out, load_sem.at[13])
    handed.start()

    acc = jnp.zeros((chans * blk, chans * blk), f32)
    for b in range(cx // blk):
        rows = pl.ds(b * blk, blk)
        acc += lax.dot_general(
            x_ref[:, rows, :].reshape(chans * blk, cy),
            gp[:, rows, :].reshape(chans * blk, cy),
            kron_dims,
            preferred_element_type=f32,
        )
    short = jnp.sum((acc * mask).reshape(chans, blk, chans * blk), axis=1)
    lane_in = lax.broadcasted_iota(jnp.int32, (chans * blk, 4 * half), 0)
    lane_out = lax.broadcasted_iota(jnp.int32, (chans * blk, 4 * half), 1)
    gather = jnp.where(lane_in // blk == lane_out, 1.0, 0.0).astype(bf16)

    def split(value):
        high = value.astype(bf16)
        rest = value - high.astype(f32)
        mid = rest.astype(bf16)
        low = (rest - mid.astype(f32)).astype(bf16)
        return high, mid, low

    sums = sum(dot(piece, gather) for piece in split(short))
    bias_sum = jnp.sum(bsum[...], axis=1, keepdims=True)
    lanes = lax.broadcasted_iota(jnp.int32, (chans, 4 * half), 1)
    terms = factor * jnp.where(lanes == chans, bias_sum, sums)
    tsend[...] = terms[:pair_rows] + pltpu.roll(terms[pair_rows:], half, 1)
    spread_terms()
    arrive(2)
    grad_spectrum = z_forward(2)
    gspec[...] = expand(grad_spectrum, 2)

    def back(k, carry):
        rows = pl.ds(pl.multiple_of(k * chans, chans), chans)
        mix[rows, :] = jnp.sum(gspec[rows, :][None] * wa[k].astype(f32), axis=1)
        return carry

    lax.fori_loop(0, modes, back, 0)
    z_inverse(3)
    ship(3)

    gout[...] = expand(grad_spectrum, 4)
    every = trecv.at[pl.ds(0, n - 1)]
    pltpu.make_async_copy(every, every, recv_sem.at[4]).wait()
    term_ref[...] = jnp.sum(trecv[...], axis=0)
    handed.wait()
    arrive(3)
    got_ref[...] = recv[3]
    for s in range(4):
        left(s)
    pltpu.make_async_copy(every, every, send_sem.at[4]).wait()


def outer_kernel(
    modes, chans, planes, factor,
    spec, gspec, term_ref, got_ref, tyi, txi, turn, local_hbm,
    dx_ref, sg_hbm, point_ref, bias_ref,
    sg_ref, sems, local, fbuf, jbuf,
):
    f32, bf16 = jnp.float32, jnp.bfloat16
    load = pltpu.make_async_copy(local_hbm, local, sems.at[modes])
    load.start()
    half = 2 * modes
    area = 2 * chans * chans

    def put(k):
        rows = pl.ds(pl.multiple_of(k * area, area), area)
        return pltpu.make_async_copy(sg_ref.at[rows], sg_hbm.at[rows], sems.at[k])

    def outer(k, carry):
        rows = pl.ds(pl.multiple_of(k * chans, chans), chans)
        scale = jnp.where(k == 0, 1.0, 2.0)
        prod = (scale * spec[rows, :])[:, None, :] * gspec[rows, :][None]
        prod = prod.reshape(chans * chans, 4 * half)
        folded = prod + pltpu.roll(prod, 2 * half, 1)
        sg_ref[pl.ds(k * area, chans * chans, stride=2), :] = folded[:, :half]
        sg_ref[pl.ds(k * area + 1, chans * chans, stride=2), :] = folded[:, half : 2 * half]
        put(k).start()
        return carry

    lax.fori_loop(0, modes, outer, 0)
    total = term_ref[...]
    joined = jnp.concatenate([total, pltpu.roll(total, 3 * half, 1)], axis=0)
    point_ref[...] = joined[:, :chans]
    row = lax.broadcasted_iota(jnp.int32, (chans, chans), 0)
    col = lax.broadcasted_iota(jnp.int32, (chans, chans), 1)
    bias_ref[...] = jnp.sum(
        jnp.where(row == col, joined[:, chans : chans + 1], 0.0), axis=0, keepdims=True
    )

    pair_rows = chans // 2
    wide = got_ref[...].astype(f32)
    flat = wide.reshape(planes * pair_rows, 4 * half).astype(bf16)
    fbuf[...] = wide
    jbuf[...] = jnp.dot(flat, turn[...], preferred_element_type=f32).reshape(
        planes, pair_rows, 4 * half
    )
    load.wait()
    cy = tyi.shape[1] // 2
    for c in range(pair_rows):
        pair = jnp.concatenate([fbuf[:, c, :], jbuf[:, c, :]], axis=0).astype(bf16)
        rows_x = jnp.dot(txi[...], pair, preferred_element_type=f32).astype(bf16)
        both = factor * jnp.dot(rows_x, tyi[...], preferred_element_type=f32)
        dx_ref[c] = (both[:, :cy] + local[c]).astype(bf16)
        dx_ref[c + pair_rows] = (both[:, cy:] + local[c + pair_rows]).astype(bf16)

    def finish(k, carry):
        put(k).wait()
        return carry

    lax.fori_loop(0, modes, finish, 0)


def fused(layer_input, cotangent, spec_weight, point_weight, bias_term):
    chans, cx, cy = layer_input.shape[2:]
    modes = spec_weight.shape[0]
    half = 2 * modes
    planes = lax.axis_size("mp")
    factor = 1.0 / math.sqrt(cx * cy * planes)
    kc = modes * chans
    rows = modes * chans * chans * 2

    def const(value):
        return jnp.asarray(np.asarray(value, np.float32).astype(ml_dtypes.bfloat16))

    cos_x, msin_x = np_table(cx, half, True)
    cos_y, msin_y = np_table(cy, half, True)
    cos_z, msin_z = np_table(planes, modes, False)
    eye = np.eye(chans // 2)
    two = np.eye(2)
    ty1 = np.kron(two, np.concatenate([cos_y, msin_y], 1))
    ty2 = np.kron(two, np.concatenate([-msin_y, cos_y], 1))
    tyi = ty1.T
    txf = np.concatenate([cos_x.T, msin_x.T], 1)
    txi = np.concatenate([cos_x, -msin_x], 1)
    kf = np.stack([np.kron(cos_z.T, eye), np.kron(msin_z.T, eye)])
    ki = np.stack([np.kron(cos_z, eye), np.kron(msin_z, eye)])
    picks = (
        [(0, 1), (1, 1), (1, 1), (0, 1)],
        [(0, 1), (1, 1), (1, -1), (0, -1)],
        [(0, 1), (0, 1), (1, 1), (1, 1)],
        [(0, 1), (1, 1), (1, 1), (0, -1)],
    )
    perm = np.stack(
        [lane_map(half, [(1, -1), (0, 1), (3, -1), (2, 1)])]
        + [lane_map(half, pick) for pick in picks]
        + [
            lane_map(half, [(0, 1), (0, 1), (0, 0), (0, 0)]),
            lane_map(half, [(0, 0), (0, 0), (0, -1), (0, 1)]),
        ]
        + [lane_map(half, [(g + 2, sign) for g, sign in pick]) for pick in picks]
    )
    mask = jnp.asarray(np.kron(np.ones((chans, chans)), np.eye(16)).astype(np.float32))
    tables = [const(t) for t in (ty1, ty2, tyi, txf, txi, kf, ki, perm)] + [mask]
    vmem = pl.BlockSpec(memory_space=pltpu.VMEM)
    hbm = pl.BlockSpec(memory_space=pltpu.HBM)
    smem = pl.BlockSpec(memory_space=pltpu.SMEM)
    f32, bf16 = jnp.float32, jnp.bfloat16
    got, local, spec, gspec, terms = pl.pallas_call(
        functools.partial(fused_kernel, planes, chans, cx, cy, modes, factor),
        out_shape=(
            jax.ShapeDtypeStruct((planes, chans // 2, 4 * half), bf16),
            jax.ShapeDtypeStruct((chans, cx, cy), f32),
            jax.ShapeDtypeStruct((kc, 4 * half), f32),
            jax.ShapeDtypeStruct((kc, 4 * half), f32),
            jax.ShapeDtypeStruct((chans // 2, 4 * half), f32),
        ),
        in_specs=[hbm] * 4 + [smem] + [hbm] * 9,
        out_specs=(vmem, hbm, vmem, vmem, vmem),
        scratch_shapes=[
            pltpu.VMEM((4, planes, chans // 2, 4 * half), bf16),
            pltpu.VMEM((4, planes, chans // 2, 4 * half), bf16),
            pltpu.VMEM((planes, chans // 2, 4 * half), f32),
            pltpu.VMEM((planes, chans // 2, 4 * half), f32),
            pltpu.VMEM((kc, 4 * half), f32),
            pltpu.VMEM((2 * chans * chans, half), f32),
            pltpu.VMEM((modes, chans, chans, 4 * half), bf16),
            pltpu.VMEM((kc, 4 * half), f32),
            pltpu.VMEM((chans, cx, cy), f32),
            pltpu.VMEM((chans, cx, cy), bf16),
            pltpu.VMEM((chans, cy), f32),
            pltpu.SemaphoreType.DMA((5,)),
            pltpu.SemaphoreType.DMA((5,)),
            pltpu.SemaphoreType.DMA((14,)),
            pltpu.VMEM((chans, cx, cy), bf16),
            pltpu.VMEM((chans, cx, cy), bf16),
            pltpu.VMEM((rows, half), bf16),
            pltpu.VMEM((chans, chans), bf16),
            pltpu.VMEM((chans // 2, 4 * half), f32),
            pltpu.VMEM((planes, chans // 2, 4 * half), f32),
        ]
        + [pltpu.VMEM(t.shape, t.dtype) for t in tables],
        compiler_params=pltpu.CompilerParams(
            collective_id=0, has_side_effects=True, vmem_limit_bytes=60 * 1024 * 1024
        ),
    )(
        layer_input.reshape(chans, cx, cy), cotangent.reshape(chans, cx, cy),
        spec_weight.reshape(rows, half), point_weight, bias_term, *tables,
    )
    dx, sg, point, bias = pl.pallas_call(
        functools.partial(outer_kernel, modes, chans, planes, factor),
        out_shape=(
            jax.ShapeDtypeStruct((chans, cx, cy), bf16),
            jax.ShapeDtypeStruct((rows, half), f32),
            jax.ShapeDtypeStruct((chans, chans), f32),
            jax.ShapeDtypeStruct((1, chans), f32),
        ),
        in_specs=[vmem] * 7 + [hbm],
        out_specs=(vmem, hbm, vmem, vmem),
        scratch_shapes=[
            pltpu.VMEM((rows, half), f32),
            pltpu.SemaphoreType.DMA((modes + 1,)),
            pltpu.VMEM((chans, cx, cy), f32),
            pltpu.VMEM((planes, chans // 2, 4 * half), f32),
            pltpu.VMEM((planes, chans // 2, 4 * half), f32),
        ],
        compiler_params=pltpu.CompilerParams(vmem_limit_bytes=60 * 1024 * 1024),
    )(spec, gspec, terms, got, tables[2], tables[4], const(perm[0]), local)
    return (
        dx.reshape(layer_input.shape),
        sg.reshape(spec_weight.shape),
        point,
        bias.reshape(chans),
    )


def shards(layer_input, cotangent, spec_weight, point_weight, bias_term):
    local_z, cells_x, cells_y = (layer_input.shape[1], layer_input.shape[3], layer_input.shape[4])
    depth_z = local_z * lax.axis_size("mp")
    channels, half = (layer_input.shape[2], 2 * spec_weight.shape[0])
    one_row = spec_weight.shape[4] == half and lax.axis_size("mp") == half
    if (
        layer_input.shape[0] == 1 and local_z == 1 and lax.axis_size("dp") == 1
        and one_row and channels == 16 and half == 32 and cells_x == cells_y == 128
    ):
        return fused(layer_input, cotangent, spec_weight, point_weight, bias_term)
    mode_count = spec_weight.shape[0]
    table_x = dft_table(cells_x, 2 * mode_count, True)
    table_y = dft_table(cells_y, 2 * mode_count, True)
    table_z = dft_table(depth_z, mode_count, False)
    factor = 1.0 / math.sqrt(cells_x * cells_y * depth_z)
    mode_scale = jnp.where(jnp.arange(mode_count) == 0, 1.0, 2.0).astype(jnp.float32)
    spectrum = to_spectrum(layer_input, table_x, table_y, table_z, factor)
    mixed_spec = mix_modes(spectrum, spec_weight, mode_scale)
    spectral = to_field(mixed_spec, table_x, table_y, table_z, factor)
    pre_act = (
        spectral
        + mixed_dot("nzixy,io->nzoxy", layer_input, point_weight)
        + bias_term[None, None, :, None, None]
    )
    grad_pre = (cotangent.astype(jnp.float32) * gelu_slope(pre_act)).astype(jnp.bfloat16)
    point_terms = factor * mixed_dot("nzixy,nzoxy->io", layer_input, grad_pre)
    bias_terms = factor * jnp.sum(grad_pre, axis=(0, 1, 3, 4), dtype=jnp.float32)
    terms = jnp.concatenate([point_terms, bias_terms[None]], axis=0)
    grad_spectrum, terms_sum = to_spectrum(
        grad_pre, table_x, table_y, table_z, factor, terms.reshape(-1)
    )
    terms_sum = lax.psum(terms_sum.reshape(terms.shape), "dp")
    point_grad, bias_grad = terms_sum[:-1], terms_sum[-1]
    back_spec = back_modes(grad_spectrum, spec_weight, mode_scale)
    input_grad = (
        to_field(back_spec, table_x, table_y, table_z, factor)
        + mixed_dot("nzoxy,io->nzixy", grad_pre, point_weight)
    ).astype(jnp.bfloat16)
    spec_grad = lax.psum(
        weight_terms(spectrum, grad_spectrum, mode_scale).astype(jnp.bfloat16), "dp"
    ).astype(jnp.float32)
    return (input_grad, spec_grad, point_grad, bias_grad)


def solution(mesh):
    placed = (
        P("dp", "mp", None, None, None),
        P("dp", "mp", None, None, None),
        P(None, None, None, None, "mp"),
        P(),
        P(),
    )
    return jax.shard_map(
        shards,
        mesh=mesh,
        in_specs=placed,
        out_specs=(P("dp", "mp", None, None, None), P(None, None, None, None, "mp"), P(), P()),
        check_vma=False,
    )
```

```python
import functools
import math

import jax
import jax.numpy as jnp
import ml_dtypes
import numpy as np
from jax import lax
from jax.experimental import pallas as pl
from jax.experimental.pallas import tpu as pltpu
from jax.sharding import PartitionSpec as P

SQRT_TWO_PI = math.sqrt(2.0 / math.pi)


def mixed_dot(formula, first_op, second_op):
    return jnp.einsum(formula, first_op, second_op, preferred_element_type=jnp.float32)


def dft_table(length, freq_count, signed):
    frequency = jnp.arange(freq_count, dtype=jnp.int32)
    if signed:
        frequency = jnp.where(frequency >= freq_count // 2, frequency - freq_count, frequency)
    places = jnp.arange(length, dtype=jnp.int32)
    phases = jnp.mod(places[:, None] * frequency[None, :], length).astype(jnp.float32) * (
        2.0 * math.pi / length
    )
    return jnp.concatenate([jnp.cos(phases), -jnp.sin(phases)], axis=1).astype(jnp.bfloat16)


def split3(value):
    high = value.astype(jnp.bfloat16)
    rest = value - high.astype(jnp.float32)
    mid = rest.astype(jnp.bfloat16)
    low = (rest - mid.astype(jnp.float32)).astype(jnp.bfloat16)
    return jnp.stack([high, mid, low])


def to_spectrum(values, table_x, table_y, table_z, factor, extra=None):
    samples, local_z, channels = (values.shape[0], values.shape[1], values.shape[2])
    half_x = table_x.shape[1] // 2
    half_y = table_y.shape[1] // 2
    half_z = table_z.shape[1] // 2
    along_y = mixed_dot("nzcxy,yk->nzcxk", values, table_y).astype(jnp.bfloat16)
    partial_value = mixed_dot("nzcxk,xa->nzcak", along_y, table_x)
    real_part = partial_value[..., :half_x, :half_y] - partial_value[..., half_x:, half_y:]
    imag_part = partial_value[..., :half_x, half_y:] + partial_value[..., half_x:, :half_y]
    planes = (
        jnp.stack([real_part, imag_part], axis=3)
        .reshape(samples, local_z, channels, 2, half_x * half_y)
        .astype(jnp.bfloat16)
    )
    shards_mp = lax.axis_size("mp")
    width = half_x * half_y // shards_mp
    total = None
    if extra is not None:
        size = extra.size
        cells = samples * local_z * channels * 2
        more = -(-3 * size // cells)
        flat = jnp.pad(split3(extra).reshape(-1), (0, cells * more - 3 * size))
        flat = jnp.broadcast_to(
            flat.reshape(samples, local_z, channels, 2, 1, more),
            (samples, local_z, channels, 2, shards_mp, more),
        )
        planes = jnp.concatenate(
            [planes.reshape(samples, local_z, channels, 2, shards_mp, width), flat], axis=5
        ).reshape(samples, local_z, channels, 2, shards_mp * (width + more))
    planes = lax.all_to_all(planes, "mp", split_axis=4, concat_axis=1, tiled=True)
    if extra is not None:
        tail = planes[..., width:].astype(jnp.float32)
        tail = tail.reshape(samples, shards_mp, local_z, channels, 2, more)
        tail = jnp.transpose(tail, (1, 0, 2, 3, 4, 5)).reshape(shards_mp, -1)
        total = jnp.sum(jnp.sum(tail, axis=0)[: 3 * size].reshape(3, size), axis=0)
        planes = planes[..., :width]
    whole_z = mixed_dot("nzcrp,zk->nkcrp", planes, table_z)
    real_z = whole_z[:, :half_z, :, 0] - whole_z[:, half_z:, :, 1]
    imag_z = whole_z[:, :half_z, :, 1] + whole_z[:, half_z:, :, 0]
    result = (factor * jnp.stack([real_z, imag_z], axis=3)).astype(jnp.bfloat16)
    return result if extra is None else (result, total)


def to_field(spectrum, table_x, table_y, table_z, factor):
    depth_z = table_z.shape[0]
    half_z = table_z.shape[1] // 2
    cells_x = table_x.shape[0]
    half_x = table_x.shape[1] // 2
    half_y = table_y.shape[1] // 2
    waves_z = table_z.reshape(depth_z, 2, half_z)
    whole_z = mixed_dot("nkcrp,zqk->nzqcrp", spectrum, waves_z)
    real_z = whole_z[:, :, 0, :, 0] + whole_z[:, :, 1, :, 1]
    imag_z = whole_z[:, :, 0, :, 1] - whole_z[:, :, 1, :, 0]
    pencil_data = jnp.stack([real_z, imag_z], axis=3).astype(jnp.bfloat16)
    waves_x = table_x.reshape(cells_x, 2, half_x)
    pencil_rows = lax.all_to_all(pencil_data, "mp", split_axis=1, concat_axis=4, tiled=True)
    samples = pencil_rows.shape[0]
    local_z = pencil_rows.shape[1]
    channels = pencil_rows.shape[2]
    mode_grid = pencil_rows.reshape(samples, local_z, channels, 2, half_x, half_y)
    along_x = mixed_dot("nzcrab,xqa->nzcxqrb", mode_grid, waves_x)
    real_x = along_x[:, :, :, :, 0, 0] + along_x[:, :, :, :, 1, 1]
    imag_x = along_x[:, :, :, :, 0, 1] - along_x[:, :, :, :, 1, 0]
    half_spec = jnp.concatenate([real_x, imag_x], axis=-1).astype(jnp.bfloat16)
    return factor * mixed_dot("nzcxk,yk->nzcxy", half_spec, table_y)


def mix_modes(spectrum, weight, mode_scale):
    formula = "nkip,kiop->nkop"
    spec_re, spec_im = (spectrum[:, :, :, 0], spectrum[:, :, :, 1])
    weight_re, weight_im = (weight[:, :, :, 0], weight[:, :, :, 1])
    real_part = mixed_dot(formula, spec_re, weight_re) - mixed_dot(formula, spec_im, weight_im)
    imag_part = mixed_dot(formula, spec_re, weight_im) + mixed_dot(formula, spec_im, weight_re)
    return (
        mode_scale[None, :, None, None, None] * jnp.stack([real_part, imag_part], axis=3)
    ).astype(jnp.bfloat16)


def back_modes(grads, weight, mode_scale):
    formula = "nkop,kiop->nkip"
    grad_re, grad_im = (grads[:, :, :, 0], grads[:, :, :, 1])
    weight_re, weight_im = (weight[:, :, :, 0], weight[:, :, :, 1])
    real_part = mixed_dot(formula, grad_re, weight_re) + mixed_dot(formula, grad_im, weight_im)
    imag_part = mixed_dot(formula, grad_im, weight_re) - mixed_dot(formula, grad_re, weight_im)
    return (
        mode_scale[None, :, None, None, None] * jnp.stack([real_part, imag_part], axis=3)
    ).astype(jnp.bfloat16)


def weight_terms(spectra, grads, mode_scale):
    formula = "nkip,nkop->kiop"
    spec_re, spec_im = (spectra[:, :, :, 0], spectra[:, :, :, 1])
    grad_re, grad_im = (grads[:, :, :, 0], grads[:, :, :, 1])
    real_part = mixed_dot(formula, spec_re, grad_re) + mixed_dot(formula, spec_im, grad_im)
    imag_part = mixed_dot(formula, spec_re, grad_im) - mixed_dot(formula, spec_im, grad_re)
    return mode_scale[:, None, None, None, None] * jnp.stack([real_part, imag_part], axis=3)


def gelu_slope(pre_act):
    inner_arg = SQRT_TWO_PI * (pre_act + 0.044715 * pre_act * pre_act * pre_act)
    tanh_val = jnp.tanh(inner_arg)
    return 0.5 * (1.0 + tanh_val) + 0.5 * pre_act * (1.0 - tanh_val * tanh_val) * SQRT_TWO_PI * (
        1.0 + 0.134145 * pre_act * pre_act
    )


def np_table(length, freq_count, signed):
    frequency = np.arange(freq_count)
    if signed:
        frequency = np.where(frequency >= freq_count // 2, frequency - freq_count, frequency)
    phases = np.mod(np.arange(length)[:, None] * frequency[None, :], length) * (
        2.0 * math.pi / length
    )
    return np.cos(phases), -np.sin(phases)


def lane_map(half, picks):
    out = np.zeros((4 * half, 4 * half))
    for group, (source, sign) in enumerate(picks):
        for lane in range(half):
            out[source * half + lane, group * half + lane] = sign
    return out


def fused_kernel(
    planes, chans, cx, cy, modes, factor,
    x_hbm, cot_hbm, w_hbm, pw_hbm, bias_ref, *rest,
):
    tables_hbm, (got_ref, point_out, spec, gout, term_ref), rest = (
        rest[:9], rest[9:14], rest[14:]
    )
    (send, recv, fbuf, jbuf, gspec, wraw, wa, mix, pwise, gp, bsum,
     send_sem, recv_sem, load_sem, x_ref, cot_ref, w_ref, pw_ref,
     tsend, trecv) = rest[:20]
    ty1, ty2, tyi, txf, txi, kf, ki, perm, mask_ref = rest[20:]
    loads = [
        pltpu.make_async_copy(source, target, load_sem.at[place])
        for place, (source, target) in enumerate(
            zip(
                (x_hbm, *(tables_hbm[t] for t in (0, 1, 3, 7, 8, 5)), w_hbm, pw_hbm,
                 cot_hbm, *(tables_hbm[t] for t in (2, 4, 6))),
                (x_ref, ty1, ty2, txf, perm, mask_ref, kf, w_ref, pw_ref,
                 cot_ref, tyi, txi, ki),
            )
        )
    ]
    for load in loads:
        load.start()
    f32, bf16 = jnp.float32, jnp.bfloat16
    me = lax.axis_index("mp")
    n = planes
    half = 2 * modes
    kc = modes * chans
    blk = 16
    pair_rows = chans // 2

    def dot(a, b):
        return jnp.dot(a, b, preferred_element_type=f32)

    barrier = pltpu.get_barrier_semaphore()

    def greet(j, carry):
        other = lax.rem(me + j, n)
        pl.semaphore_signal(
            barrier, inc=1, device_id={"mp": other}, device_id_type=pl.DeviceIdType.MESH
        )
        return carry

    lax.fori_loop(1, n, greet, 0)

    def ship(s):
        def go(j, carry):
            other = lax.rem(me + j, n)
            pltpu.make_async_remote_copy(
                src_ref=send.at[s, other],
                dst_ref=recv.at[s, me],
                send_sem=send_sem.at[s],
                recv_sem=recv_sem.at[s],
                device_id={"mp": other},
                device_id_type=pl.DeviceIdType.MESH,
            ).start()
            return carry

        lax.fori_loop(1, n, go, 0)
        recv[s, me] = send[s, me]

    def spread_terms():
        def go(j, carry):
            other = lax.rem(me + j, n)
            pltpu.make_async_remote_copy(
                src_ref=tsend,
                dst_ref=trecv.at[me],
                send_sem=send_sem.at[4],
                recv_sem=recv_sem.at[4],
                device_id={"mp": other},
                device_id_type=pl.DeviceIdType.MESH,
            ).start()
            return carry

        lax.fori_loop(1, n, go, 0)
        trecv[me] = tsend[...]

    def arrive(s):
        part = recv.at[s, pl.ds(0, n - 1)]
        pltpu.make_async_copy(part, part, recv_sem.at[s]).wait()

    def left(s):
        part = send.at[s, pl.ds(0, n - 1)]
        pltpu.make_async_copy(part, part, send_sem.at[s]).wait()

    def forward(src_ref, c):
        plane = jnp.concatenate([src_ref[c], src_ref[c + pair_rows]], axis=1)
        stacked = jnp.concatenate(
            [dot(plane, ty1[...]).astype(bf16), dot(plane, ty2[...]).astype(bf16)], axis=0
        )
        fbuf[:, c, :] = dot(txf[...], stacked)

    for load in loads[:4]:
        load.wait()
    for c in range(pair_rows):
        forward(x_ref, c)
    send[0] = fbuf[...].astype(bf16)
    pl.semaphore_wait(barrier, n - 1)
    ship(0)

    for load in loads[4:]:
        load.wait()

    def spread(k, carry):
        rows = chans * chans
        start = k * (2 * rows)
        wraw[...] = w_ref[pl.ds(pl.multiple_of(start, 2 * rows), 2 * rows), :].astype(f32)
        real = wraw[pl.ds(0, rows, stride=2), :].astype(bf16)
        imag = wraw[pl.ds(1, rows, stride=2), :].astype(bf16)
        wa[k] = (dot(real, perm[5][:half]) + dot(imag, perm[6][:half])).astype(bf16).reshape(
            chans, chans, 4 * half
        )
        return carry

    lax.fori_loop(0, modes, spread, 0)

    row = lax.broadcasted_iota(jnp.int32, (chans * blk, chans), 0)
    col = lax.broadcasted_iota(jnp.int32, (chans * blk, chans), 1)
    rep = jnp.where(row // blk == col, 1.0, 0.0).astype(bf16)
    mask = mask_ref[...]
    kron_dims = (((1,), (1,)), ((), ()))

    def kron(transposed):
        if transposed:
            tall = lax.dot_general(rep, pw_ref[...], kron_dims, preferred_element_type=f32)
        else:
            tall = dot(rep, pw_ref[...])
        wide = lax.dot_general(tall.astype(bf16), rep, kron_dims, preferred_element_type=f32)
        return (wide * mask).astype(bf16)

    def pointwise(src_ref, matrix):
        for b in range(cx // blk):
            rows = pl.ds(b * blk, blk)
            block = src_ref[:, rows, :].reshape(chans * blk, cy)
            pwise[:, rows, :] = dot(matrix, block).reshape(chans, blk, cy)

    pointwise(x_ref, kron(True))

    def z_forward(s):
        got = recv[s].astype(f32).reshape(n * pair_rows, 4 * half).astype(bf16)
        turned = dot(got, perm[0]).astype(bf16)
        return (factor * (dot(kf[0], got) + dot(kf[1], turned))).astype(bf16)

    def z_inverse(s):
        folded = mix[...] + pltpu.roll(mix[...], 2 * half, 1)
        scale = jnp.where(
            lax.broadcasted_iota(jnp.int32, (kc, 4 * half), 0) < chans, 1.0, 2.0
        )
        folded = (scale * folded).reshape(modes, chans, 4 * half)
        lane = lax.broadcasted_iota(jnp.int32, (modes, pair_rows, 4 * half), 2)
        packed = jnp.where(lane < 2 * half, folded[:, :pair_rows], folded[:, pair_rows:])
        modes_in = packed.reshape(modes * pair_rows, 4 * half).astype(bf16)
        turned = dot(modes_in, perm[0]).astype(bf16)
        out = dot(ki[0], modes_in) - dot(ki[1], turned)
        send[s] = out.reshape(n, pair_rows, 4 * half).astype(bf16)

    def prepare_inverse(s):
        wide = recv[s].astype(f32)
        got = wide.reshape(n * pair_rows, 4 * half).astype(bf16)
        fbuf[...] = wide
        jbuf[...] = dot(got, perm[0]).reshape(n, pair_rows, 4 * half)

    def inverse(c):
        pair = jnp.concatenate([fbuf[:, c, :], jbuf[:, c, :]], axis=0).astype(bf16)
        lines = dot(txi[...], pair).astype(bf16)
        both = factor * dot(lines, tyi[...])
        return ((c, both[:, :cy]), (c + pair_rows, both[:, cy:]))

    def expand(values, which):
        parts = [
            dot(values, perm[which + 6 * h]).reshape(modes, pair_rows, 4 * half)
            for h in range(2)
        ]
        return jnp.concatenate(parts, axis=1).reshape(kc, 4 * half)

    arrive(0)
    spectrum = z_forward(0)
    gspec[...] = expand(spectrum, 1)

    def mixing(k, carry):
        rows = pl.ds(pl.multiple_of(k * chans, chans), chans)
        left_part = gspec[rows, :]
        mix[rows, :] = jnp.sum(left_part[:, None, :] * wa[k].astype(f32), axis=0)
        return carry

    lax.fori_loop(0, modes, mixing, 0, unroll=True)
    z_inverse(1)
    ship(1)
    spec[...] = expand(spectrum, 3)
    arrive(1)
    prepare_inverse(1)
    for c, spectral in (item for p in range(pair_rows) for item in inverse(p)):
        pre = spectral + pwise[c] + bias_ref[c]
        squared = pre * pre
        tanh_val = jnp.tanh(SQRT_TWO_PI * pre * (1.0 + 0.044715 * squared))
        slope = 0.5 * (1.0 + tanh_val) + (0.5 * SQRT_TWO_PI) * pre * (
            1.0 - tanh_val * tanh_val
        ) * (1.0 + 0.134145 * squared)
        grad = (cot_ref[c].astype(f32) * slope).astype(bf16)
        gp[c] = grad
        bsum[pl.ds(c, 1), :] = jnp.sum(grad.astype(f32), axis=0, keepdims=True)
    for c in range(pair_rows):
        forward(gp, c)
    send[2] = fbuf[...].astype(bf16)
    ship(2)
    pointwise(gp, kron(False))
    handed = pltpu.make_async_copy(pwise, point_out, load_sem.at[13])
    handed.start()

    acc = jnp.zeros((chans * blk, chans * blk), f32)
    for b in range(cx // blk):
        rows = pl.ds(b * blk, blk)
        acc += lax.dot_general(
            x_ref[:, rows, :].reshape(chans * blk, cy),
            gp[:, rows, :].reshape(chans * blk, cy),
            kron_dims,
            preferred_element_type=f32,
        )
    short = jnp.sum((acc * mask).reshape(chans, blk, chans * blk), axis=1)
    lane_in = lax.broadcasted_iota(jnp.int32, (chans * blk, 4 * half), 0)
    lane_out = lax.broadcasted_iota(jnp.int32, (chans * blk, 4 * half), 1)
    gather = jnp.where(lane_in // blk == lane_out, 1.0, 0.0).astype(bf16)

    def split(value):
        high = value.astype(bf16)
        rest = value - high.astype(f32)
        mid = rest.astype(bf16)
        low = (rest - mid.astype(f32)).astype(bf16)
        return high, mid, low

    sums = sum(dot(piece, gather) for piece in split(short))
    bias_sum = jnp.sum(bsum[...], axis=1, keepdims=True)
    lanes = lax.broadcasted_iota(jnp.int32, (chans, 4 * half), 1)
    terms = factor * jnp.where(lanes == chans, bias_sum, sums)
    tsend[...] = terms[:pair_rows] + pltpu.roll(terms[pair_rows:], half, 1)
    spread_terms()
    arrive(2)
    grad_spectrum = z_forward(2)
    gspec[...] = expand(grad_spectrum, 2)

    def back(k, carry):
        rows = pl.ds(pl.multiple_of(k * chans, chans), chans)
        mix[rows, :] = jnp.sum(gspec[rows, :][None] * wa[k].astype(f32), axis=1)
        return carry

    lax.fori_loop(0, modes, back, 0, unroll=True)
    z_inverse(3)
    ship(3)

    gout[...] = expand(grad_spectrum, 4)
    every = trecv.at[pl.ds(0, n - 1)]
    pltpu.make_async_copy(every, every, recv_sem.at[4]).wait()
    term_ref[...] = jnp.sum(trecv[...], axis=0)
    handed.wait()
    arrive(3)
    got_ref[...] = recv[3]
    for s in range(4):
        left(s)
    pltpu.make_async_copy(every, every, send_sem.at[4]).wait()


def outer_kernel(
    modes, chans, planes, factor,
    spec, gspec, term_ref, got_ref, tyi, txi, turn, local_hbm,
    dx_ref, sg_hbm, point_ref, bias_ref,
    sg_ref, sems, local, fbuf, jbuf,
):
    f32, bf16 = jnp.float32, jnp.bfloat16
    load = pltpu.make_async_copy(local_hbm, local, sems.at[modes])
    load.start()
    half = 2 * modes
    area = 2 * chans * chans

    def put(k):
        rows = pl.ds(pl.multiple_of(k * area, area), area)
        return pltpu.make_async_copy(sg_ref.at[rows], sg_hbm.at[rows], sems.at[k])

    def outer(k, carry):
        rows = pl.ds(pl.multiple_of(k * chans, chans), chans)
        scale = jnp.where(k == 0, 1.0, 2.0)
        prod = (scale * spec[rows, :])[:, None, :] * gspec[rows, :][None]
        prod = prod.reshape(chans * chans, 4 * half)
        folded = prod + pltpu.roll(prod, 2 * half, 1)
        sg_ref[pl.ds(k * area, chans * chans, stride=2), :] = folded[:, :half]
        sg_ref[pl.ds(k * area + 1, chans * chans, stride=2), :] = folded[:, half : 2 * half]
        put(k).start()
        return carry

    lax.fori_loop(0, modes, outer, 0, unroll=True)
    total = term_ref[...]
    joined = jnp.concatenate([total, pltpu.roll(total, 3 * half, 1)], axis=0)
    point_ref[...] = joined[:, :chans]
    row = lax.broadcasted_iota(jnp.int32, (chans, chans), 0)
    col = lax.broadcasted_iota(jnp.int32, (chans, chans), 1)
    bias_ref[...] = jnp.sum(
        jnp.where(row == col, joined[:, chans : chans + 1], 0.0), axis=0, keepdims=True
    )

    pair_rows = chans // 2
    wide = got_ref[...].astype(f32)
    flat = wide.reshape(planes * pair_rows, 4 * half).astype(bf16)
    fbuf[...] = wide
    jbuf[...] = jnp.dot(flat, turn[...], preferred_element_type=f32).reshape(
        planes, pair_rows, 4 * half
    )
    load.wait()
    cy = tyi.shape[1] // 2
    for c in range(pair_rows):
        pair = jnp.concatenate([fbuf[:, c, :], jbuf[:, c, :]], axis=0).astype(bf16)
        rows_x = jnp.dot(txi[...], pair, preferred_element_type=f32).astype(bf16)
        both = factor * jnp.dot(rows_x, tyi[...], preferred_element_type=f32)
        dx_ref[c] = (both[:, :cy] + local[c]).astype(bf16)
        dx_ref[c + pair_rows] = (both[:, cy:] + local[c + pair_rows]).astype(bf16)

    def finish(k, carry):
        put(k).wait()
        return carry

    lax.fori_loop(0, modes, finish, 0)


def fused(layer_input, cotangent, spec_weight, point_weight, bias_term):
    chans, cx, cy = layer_input.shape[2:]
    modes = spec_weight.shape[0]
    half = 2 * modes
    planes = lax.axis_size("mp")
    factor = 1.0 / math.sqrt(cx * cy * planes)
    kc = modes * chans
    rows = modes * chans * chans * 2

    def const(value):
        return jnp.asarray(np.asarray(value, np.float32).astype(ml_dtypes.bfloat16))

    cos_x, msin_x = np_table(cx, half, True)
    cos_y, msin_y = np_table(cy, half, True)
    cos_z, msin_z = np_table(planes, modes, False)
    eye = np.eye(chans // 2)
    two = np.eye(2)
    ty1 = np.kron(two, np.concatenate([cos_y, msin_y], 1))
    ty2 = np.kron(two, np.concatenate([-msin_y, cos_y], 1))
    tyi = ty1.T
    txf = np.concatenate([cos_x.T, msin_x.T], 1)
    txi = np.concatenate([cos_x, -msin_x], 1)
    kf = np.stack([np.kron(cos_z.T, eye), np.kron(msin_z.T, eye)])
    ki = np.stack([np.kron(cos_z, eye), np.kron(msin_z, eye)])
    picks = (
        [(0, 1), (1, 1), (1, 1), (0, 1)],
        [(0, 1), (1, 1), (1, -1), (0, -1)],
        [(0, 1), (0, 1), (1, 1), (1, 1)],
        [(0, 1), (1, 1), (1, 1), (0, -1)],
    )
    perm = np.stack(
        [lane_map(half, [(1, -1), (0, 1), (3, -1), (2, 1)])]
        + [lane_map(half, pick) for pick in picks]
        + [
            lane_map(half, [(0, 1), (0, 1), (0, 0), (0, 0)]),
            lane_map(half, [(0, 0), (0, 0), (0, -1), (0, 1)]),
        ]
        + [lane_map(half, [(g + 2, sign) for g, sign in pick]) for pick in picks]
    )
    mask = jnp.asarray(np.kron(np.ones((chans, chans)), np.eye(16)).astype(np.float32))
    tables = [const(t) for t in (ty1, ty2, tyi, txf, txi, kf, ki, perm)] + [mask]
    vmem = pl.BlockSpec(memory_space=pltpu.VMEM)
    hbm = pl.BlockSpec(memory_space=pltpu.HBM)
    smem = pl.BlockSpec(memory_space=pltpu.SMEM)
    f32, bf16 = jnp.float32, jnp.bfloat16
    got, local, spec, gspec, terms = pl.pallas_call(
        functools.partial(fused_kernel, planes, chans, cx, cy, modes, factor),
        out_shape=(
            jax.ShapeDtypeStruct((planes, chans // 2, 4 * half), bf16),
            jax.ShapeDtypeStruct((chans, cx, cy), f32),
            jax.ShapeDtypeStruct((kc, 4 * half), f32),
            jax.ShapeDtypeStruct((kc, 4 * half), f32),
            jax.ShapeDtypeStruct((chans // 2, 4 * half), f32),
        ),
        in_specs=[hbm] * 4 + [smem] + [hbm] * 9,
        out_specs=(vmem, hbm, vmem, vmem, vmem),
        scratch_shapes=[
            pltpu.VMEM((4, planes, chans // 2, 4 * half), bf16),
            pltpu.VMEM((4, planes, chans // 2, 4 * half), bf16),
            pltpu.VMEM((planes, chans // 2, 4 * half), f32),
            pltpu.VMEM((planes, chans // 2, 4 * half), f32),
            pltpu.VMEM((kc, 4 * half), f32),
            pltpu.VMEM((2 * chans * chans, half), f32),
            pltpu.VMEM((modes, chans, chans, 4 * half), bf16),
            pltpu.VMEM((kc, 4 * half), f32),
            pltpu.VMEM((chans, cx, cy), f32),
            pltpu.VMEM((chans, cx, cy), bf16),
            pltpu.VMEM((chans, cy), f32),
            pltpu.SemaphoreType.DMA((5,)),
            pltpu.SemaphoreType.DMA((5,)),
            pltpu.SemaphoreType.DMA((14,)),
            pltpu.VMEM((chans, cx, cy), bf16),
            pltpu.VMEM((chans, cx, cy), bf16),
            pltpu.VMEM((rows, half), bf16),
            pltpu.VMEM((chans, chans), bf16),
            pltpu.VMEM((chans // 2, 4 * half), f32),
            pltpu.VMEM((planes, chans // 2, 4 * half), f32),
        ]
        + [pltpu.VMEM(t.shape, t.dtype) for t in tables],
        compiler_params=pltpu.CompilerParams(
            collective_id=0, has_side_effects=True, vmem_limit_bytes=60 * 1024 * 1024
        ),
    )(
        layer_input.reshape(chans, cx, cy), cotangent.reshape(chans, cx, cy),
        spec_weight.reshape(rows, half), point_weight, bias_term, *tables,
    )
    dx, sg, point, bias = pl.pallas_call(
        functools.partial(outer_kernel, modes, chans, planes, factor),
        out_shape=(
            jax.ShapeDtypeStruct((chans, cx, cy), bf16),
            jax.ShapeDtypeStruct((rows, half), f32),
            jax.ShapeDtypeStruct((chans, chans), f32),
            jax.ShapeDtypeStruct((1, chans), f32),
        ),
        in_specs=[vmem] * 7 + [hbm],
        out_specs=(vmem, hbm, vmem, vmem),
        scratch_shapes=[
            pltpu.VMEM((rows, half), f32),
            pltpu.SemaphoreType.DMA((modes + 1,)),
            pltpu.VMEM((chans, cx, cy), f32),
            pltpu.VMEM((planes, chans // 2, 4 * half), f32),
            pltpu.VMEM((planes, chans // 2, 4 * half), f32),
        ],
        compiler_params=pltpu.CompilerParams(vmem_limit_bytes=60 * 1024 * 1024),
    )(spec, gspec, terms, got, tables[2], tables[4], const(perm[0]), local)
    return (
        dx.reshape(layer_input.shape),
        sg.reshape(spec_weight.shape),
        point,
        bias.reshape(chans),
    )


def shards(layer_input, cotangent, spec_weight, point_weight, bias_term):
    local_z, cells_x, cells_y = (layer_input.shape[1], layer_input.shape[3], layer_input.shape[4])
    depth_z = local_z * lax.axis_size("mp")
    channels, half = (layer_input.shape[2], 2 * spec_weight.shape[0])
    one_row = spec_weight.shape[4] == half and lax.axis_size("mp") == half
    if (
        layer_input.shape[0] == 1 and local_z == 1 and lax.axis_size("dp") == 1
        and one_row and channels == 16 and half == 32 and cells_x == cells_y == 128
    ):
        return fused(layer_input, cotangent, spec_weight, point_weight, bias_term)
    mode_count = spec_weight.shape[0]
    table_x = dft_table(cells_x, 2 * mode_count, True)
    table_y = dft_table(cells_y, 2 * mode_count, True)
    table_z = dft_table(depth_z, mode_count, False)
    factor = 1.0 / math.sqrt(cells_x * cells_y * depth_z)
    mode_scale = jnp.where(jnp.arange(mode_count) == 0, 1.0, 2.0).astype(jnp.float32)
    spectrum = to_spectrum(layer_input, table_x, table_y, table_z, factor)
    mixed_spec = mix_modes(spectrum, spec_weight, mode_scale)
    spectral = to_field(mixed_spec, table_x, table_y, table_z, factor)
    pre_act = (
        spectral
        + mixed_dot("nzixy,io->nzoxy", layer_input, point_weight)
        + bias_term[None, None, :, None, None]
    )
    grad_pre = (cotangent.astype(jnp.float32) * gelu_slope(pre_act)).astype(jnp.bfloat16)
    point_terms = factor * mixed_dot("nzixy,nzoxy->io", layer_input, grad_pre)
    bias_terms = factor * jnp.sum(grad_pre, axis=(0, 1, 3, 4), dtype=jnp.float32)
    terms = jnp.concatenate([point_terms, bias_terms[None]], axis=0)
    grad_spectrum, terms_sum = to_spectrum(
        grad_pre, table_x, table_y, table_z, factor, terms.reshape(-1)
    )
    terms_sum = lax.psum(terms_sum.reshape(terms.shape), "dp")
    point_grad, bias_grad = terms_sum[:-1], terms_sum[-1]
    back_spec = back_modes(grad_spectrum, spec_weight, mode_scale)
    input_grad = (
        to_field(back_spec, table_x, table_y, table_z, factor)
        + mixed_dot("nzoxy,io->nzixy", grad_pre, point_weight)
    ).astype(jnp.bfloat16)
    spec_grad = lax.psum(
        weight_terms(spectrum, grad_spectrum, mode_scale).astype(jnp.bfloat16), "dp"
    ).astype(jnp.float32)
    return (input_grad, spec_grad, point_grad, bias_grad)


def solution(mesh):
    placed = (
        P("dp", "mp", None, None, None),
        P("dp", "mp", None, None, None),
        P(None, None, None, None, "mp"),
        P(),
        P(),
    )
    return jax.shard_map(
        shards,
        mesh=mesh,
        in_specs=placed,
        out_specs=(P("dp", "mp", None, None, None), P(None, None, None, None, "mp"), P(), P()),
        check_vma=False,
    )
```
